512 devices in a mesh: gx: 16 (over x, z_lo), gy: 32 (over z_hi, y, core).
Axes of the slice: x: 4, y: 4, z: 16 (z_hi: 4, z_lo: 4; z = z_hi * 4 + z_lo), core: 2. Of those that a mesh axis runs over, the one named last changes fastest.
Arguments:
- snapshot: float32 [512, 512, 384], P('gx', 'gy'), may hold values from -32 to 32
- start_one: float32 [512, 96], replicated, may hold values from -4 to 4
- start_two: float32 [512, 96], replicated, may hold values from -4 to 4
Outputs:
- basis_one: float32 [512, 96], replicated
- basis_two: float32 [512, 96], replicated
- core_tensor: float32 [96, 96, 384], P('gx', 'gy')
The draws below stay inside these ranges and needn't reach their ends.
All inputs are finite; a program needn't handle non-finite values.
Results may differ from the reference program's by a relative error of at most 0.0003.
Values sent between devices are 32-bit elements; how exact they have to be, the bound alone decides.
A program may use at most 64 MiB of HBM per device.

```python
import math
import jax
import jax.numpy as jnp
from jax import lax

I1 = 512
I2 = 512
CHAN = 12
I3 = 32
RANK = 96
ITERS = 6


def draw_snapshot(key, part):
    key = jax.random.fold_in(key, 11)
    subkeys = jax.random.split(key, 6)
    columns = CHAN * I3
    lowest, highest = (0.5, 2.0)
    row_scale = jnp.exp(jax.random.uniform(subkeys[0], (I1,), jnp.float32, math.log(lowest), math.log(highest)))
    col_scale = jnp.exp(jax.random.uniform(subkeys[1], (I2,), jnp.float32, math.log(lowest), math.log(highest)))
    common = jax.random.truncated_normal(subkeys[2], -3.0, 3.0, (I1,), jnp.float32) * (2.0 / math.sqrt(I1))
    weight_col = jnp.exp(jax.random.uniform(subkeys[3], (I2,), jnp.float32, math.log(0.3), math.log(3.0)))
    rough_part = jax.random.truncated_normal(subkeys[4], -4.0, 4.0, (I1, I2, columns), jnp.float32)
    shared = jax.random.truncated_normal(subkeys[5], -4.0, 4.0, (I2, columns), jnp.float32)
    result = row_scale[:, None, None] * col_scale[None, :, None] * rough_part
    result = result + common[:, None, None] * weight_col[None, :, None] * shared[None, :, :]
    return result.astype(jnp.float32)


def gaussian(key, dims, scale, limit, dtype=jnp.bfloat16):
    array = jax.random.normal(key, dims, jnp.float32) * scale
    return jnp.minimum(jnp.maximum(array, -limit), limit).astype(dtype)


def setup_inputs(seed: int = 0) -> dict:
    splits = jax.random.split(jax.random.key(seed), 4)
    return {
        "snapshot": draw_snapshot(jax.random.fold_in(splits[3], 71), 0),
        "start_one": gaussian(splits[1], (I1, RANK), 1.0, 4.0, jnp.float32),
        "start_two": gaussian(splits[2], (I2, RANK), 1.0, 4.0, jnp.float32),
    }


precise = lax.Precision.HIGHEST

def refine(gram_full, initial):
    vectors = initial
    for sweep_index in range(ITERS):
        images = jnp.dot(gram_full, vectors, precision=precise)
        cross_gram = jnp.dot(images.T, images, precision=precise)
        factor = jnp.linalg.cholesky(cross_gram)
        vectors = lax.linalg.triangular_solve(factor, images, left_side=False, lower=True, transpose_a=True)
    return vectors

def reference(snapshot, start_one, start_two):
    unfolded = snapshot.reshape(I1, I2 * CHAN * I3)
    gram_one = jnp.dot(unfolded, unfolded.T, precision=precise) / (I2 * CHAN * I3)
    basis_one = refine(gram_one, start_one)
    shrunk = jnp.dot(basis_one.T, unfolded, precision=precise).reshape(RANK, I2, CHAN * I3)
    unfolded_two = jnp.transpose(shrunk, (1, 0, 2)).reshape(I2, RANK * CHAN * I3)
    gram_two = jnp.dot(unfolded_two, unfolded_two.T, precision=precise) / (RANK * CHAN * I3)
    basis_two = refine(gram_two, start_two)
    core_tensor = jnp.einsum('jb,ajr->abr', basis_two, shrunk, precision=precise)
    return (basis_one, basis_two, core_tensor)
```

```python
import functools

import jax
import jax.numpy as jnp
from jax import lax
from jax.experimental import pallas as pl
from jax.experimental.pallas import tpu as pltpu
from jax.sharding import PartitionSpec as P

I1 = 512
I2 = 512
COLS = 384
RANK = 96
ITERS = 6
GX = 16
GY = 32
NX = 4
NY = 4
NZ = 16
BLOCKS = [(p, q) for p in range(4) for q in range(p, 4)]
GROWS = 128 * len(BLOCKS)
HALF = GROWS // 2
PIECE = HALF // 16
OWNERS = (0, 3, 6, 9, 12)
COLS_TWO = 6 * COLS // GY

MESH = pl.DeviceIdType.MESH
precise = lax.Precision.HIGHEST


def place():
    gx = lax.axis_index("gx")
    gy = lax.axis_index("gy")
    x, z_lo = lax.div(gx, 4), lax.rem(gx, 4)
    z_hi = lax.div(gy, 8)
    y = lax.rem(lax.div(gy, 2), 4)
    core = lax.rem(gy, 2)
    return gx, gy, x, y, z_hi, z_lo, core


def remote(src, dst, send, recv, target):
    return pltpu.make_async_remote_copy(
        src_ref=src, dst_ref=dst, send_sem=send, recv_sem=recv, device_id=target, device_id_type=MESH
    )


def gx_peer(d):
    gx, gy = place()[:2]
    return (lax.rem(gx + d, GX), gy)


def gy_peer(d):
    gx, gy = place()[:2]
    return (gx, lax.rem(gy + d, GY))


def sibling():
    gx, gy, *_, core = place()
    return (gx, gy + 1 - 2 * core)


def xy_peer(dx, dy):
    gx, gy, x, y, z_hi, z_lo, core = place()
    px, py = lax.rem(x + dx, NX), lax.rem(y + dy, NY)
    return (px * 4 + z_lo, z_hi * 8 + py * 2 + core), px * 4 + py


def z_peer(z):
    gx, gy, x, y, z_hi, z_lo, core = place()
    return (x * 4 + z % 4, (z // 4) * 8 + y * 2 + core)


def zz_peer(dh, dl):
    gx, gy, x, y, z_hi, z_lo, core = place()
    return (x * 4 + lax.rem(z_lo + dl, 4), lax.rem(z_hi + dh, 4) * 8 + y * 2 + core)


def meet(peers):
    barrier = pltpu.get_barrier_semaphore()
    for peer in peers:
        pl.semaphore_signal(barrier, inc=1, device_id=peer, device_id_type=MESH)
    pl.semaphore_wait(barrier, len(peers))


XY = [(dx, dy) for dx in range(NX) for dy in range(NY) if (dx, dy) != (0, 0)]


def all_reduce(gp, total, s):
    gx, gy, x, y, z_hi, z_lo, core = place()
    z = z_hi * 4 + z_lo
    mine = pl.multiple_of(core * HALF, 8)
    other = pl.multiple_of((1 - core) * HALF, 8)
    done = []
    copy = remote(gp.at[pl.ds(other, HALF)], s["rc"], s["c1s"], s["c1r"], sibling())
    copy.start()
    copy.wait_recv()
    done.append(copy)
    s["h"][...] = gp[pl.ds(mine, HALF)] + s["rc"][...]
    copies = []
    for o, (dx, dy) in enumerate(XY):
        peer, q = xy_peer(dx, dy)
        copy = remote(
            s["h"].at[pl.ds(pl.multiple_of(q * PIECE, 8), PIECE)],
            s["rxy"].at[o], s["x1s"].at[o], s["x1r"].at[o], peer,
        )
        copy.start()
        copies.append(copy)
    me = x * 4 + y
    acc = s["h"][pl.ds(pl.multiple_of(me * PIECE, 8), PIECE)]
    for o, copy in enumerate(copies):
        copy.wait_recv()
        acc = acc + s["rxy"][o]
    s["acc"][...] = acc
    done += copies
    def rows(w):
        return pl.ds(8 * w, 8)

    def to_owner(w):
        zw = OWNERS[w]
        return remote(s["acc"].at[rows(w)], s["rz"].at[z], s["z1s"].at[w], s["z1r"].at[z], z_peer(zw))

    def from_owner(w, target):
        return remote(s["agz"].at[rows(w)], s["agz"].at[rows(w)], s["z2s"].at[target], s["z2r"].at[w], z_peer(target))

    for w, zw in enumerate(OWNERS):
        @pl.when(z != zw)
        def _(w=w):
            to_owner(w).start()
    for w, zw in enumerate(OWNERS):
        @pl.when(z == zw)
        def _(w=w, zw=zw):
            part = s["acc"][rows(w)]
            others = [i for i in range(NZ) if i != zw]
            for i in others:
                remote(s["acc"].at[rows(w)], s["rz"].at[i], s["z1s"].at[w], s["z1r"].at[i], z_peer(i)).wait_recv()
                part = part + s["rz"][i]
            s["agz"][rows(w)] = part
            for i in others:
                from_owner(w, i).start()
    for w, zw in enumerate(OWNERS):
        @pl.when(z != zw)
        def _(w=w, zw=zw):
            from_owner(w, zw).wait_recv()
    own = pl.ds(pl.multiple_of(mine + me * PIECE, 8), PIECE)
    copies = []
    for o, (dx, dy) in enumerate(XY):
        peer, q = xy_peer(dx, dy)
        copy = remote(s["agz"], total.at[own], s["x2s"].at[o], s["x2r"].at[o], peer)
        copy.start()
        copies.append(copy)
    total[own] = s["agz"][...]
    for copy in copies:
        copy.wait_recv()
    done += copies
    copy = remote(total.at[pl.ds(mine, HALF)], total.at[pl.ds(mine, HALF)], s["c2s"], s["c2r"], sibling())
    copy.start()
    copy.wait_recv()
    done.append(copy)
    for copy in done:
        copy.wait_send()
    for w, zw in enumerate(OWNERS):
        @pl.when(z != zw)
        def _(w=w):
            to_owner(w).wait_send()

        @pl.when(z == zw)
        def _(w=w, zw=zw):
            for i in range(NZ):
                if i != zw:
                    from_owner(w, i).wait_send()


DMA = pltpu.SemaphoreType.DMA
REDUCE = dict(
    gp=pltpu.VMEM((GROWS, 128), jnp.float32),
    total=pltpu.VMEM((GROWS, 128), jnp.float32),
    rc=pltpu.VMEM((HALF, 128), jnp.float32),
    h=pltpu.VMEM((HALF, 128), jnp.float32),
    rxy=pltpu.VMEM((15, PIECE, 128), jnp.float32),
    acc=pltpu.VMEM((PIECE, 128), jnp.float32),
    rz=pltpu.VMEM((NZ, 8, 128), jnp.float32),
    agz=pltpu.VMEM((PIECE, 128), jnp.float32),
    c1s=DMA, c1r=DMA, c2s=DMA, c2r=DMA,
    x1s=DMA((15,)), x1r=DMA((15,)), x2s=DMA((15,)), x2r=DMA((15,)),
    z1s=DMA((5,)), z1r=DMA((NZ,)), z2s=DMA((NZ,)), z2r=DMA((5,)),
)


def gram_blocks(flat, gp):
    n = 0
    for p in range(4):
        strip = lax.dot_general(
            flat[128 * p : 128 * (p + 1)], flat[128 * p :], (((1,), (1,)), ((), ())),
            precision=precise, preferred_element_type=jnp.float32,
        )
        for q in range(4 - p):
            gp[128 * n : 128 * (n + 1)] = strip[:, 128 * q : 128 * (q + 1)]
            n += 1


def reduce_peers():
    peers = [xy_peer(dx, dy)[0] for dx in range(1, NX) for dy in range(1, NY)]
    return peers + [zz_peer(a, b) for a in range(1, 4) for b in range(1, 4)]


def first_kernel(x_ref, fib_ref, g_ref, scratch):
    s = scratch
    gx, gy, *_ = place()
    meet([gx_peer(d) for d in range(1, GX)] + [gy_peer(d) for d in range(1, GY)] + reduce_peers())
    for j in range(GX):
        s["xs"][j] = x_ref[:, j, :]
    copies = []
    for d in range(1, GX):
        peer = gx_peer(d)
        copy = remote(s["xs"].at[peer[0]], s["fib"].at[gx], s["as"].at[d - 1], s["ar"].at[d - 1], peer)
        copy.start()
        copies.append(copy)
    s["fib"][gx] = s["xs"][gx]
    for copy in copies:
        copy.wait_recv()
    flat = s["fib"][...].reshape(I1, COLS)
    fib_ref[...] = flat
    gram_blocks(flat, s["gp"])
    all_reduce(s["gp"], s["total"], s)
    g_ref[...] = s["total"][...]
    for copy in copies:
        copy.wait_send()


def second_kernel(bt_ref, fib_ref, f2_ref, g_ref, scratch):
    s = scratch
    gx, gy, *_ = place()
    meet([gx_peer(d) for d in range(1, GX)] + [gy_peer(d) for d in range(1, GY)] + reduce_peers())
    shrunk = lax.dot_general(
        bt_ref[...], fib_ref[...], (((1,), (0,)), ((), ())), precision=precise, preferred_element_type=jnp.float32
    )
    for g in range(GX):
        s["ss"][g, 0:6] = shrunk[6 * g : 6 * (g + 1)]
        s["ss"][g, 6:8] = jnp.zeros((2, COLS), jnp.float32)
    copies = []
    for d in range(1, GX):
        peer = gx_peer(d)
        copy = remote(s["ss"].at[peer[0]], s["rs"].at[gx], s["as"].at[d - 1], s["ar"].at[d - 1], peer)
        copy.start()
        copies.append(copy)
    s["rs"][gx] = s["ss"][gx]
    for copy in copies:
        copy.wait_recv()
    wide = jnp.concatenate([s["rs"][:, a, :] for a in range(6)], axis=1)
    pad = jnp.zeros((GX, 128 - COLS_TWO), jnp.float32)
    for u in range(GY):
        s["st"][u] = jnp.concatenate([wide[:, COLS_TWO * u : COLS_TWO * (u + 1)], pad], axis=1)
    seconds = []
    for d in range(1, GY):
        peer = gy_peer(d)
        copy = remote(s["st"].at[peer[1]], s["f2"].at[gy], s["bs"].at[d - 1], s["br"].at[d - 1], peer)
        copy.start()
        seconds.append(copy)
    s["f2"][gy] = s["st"][gy]
    for copy in seconds:
        copy.wait_recv()
    flat = s["f2"][...].reshape(I2, 128)
    f2_ref[...] = flat
    gram_blocks(flat, s["gp"])
    all_reduce(s["gp"], s["total"], s)
    g_ref[...] = s["total"][...]
    for copy in copies + seconds:
        copy.wait_send()


def third_kernel(bt_ref, f2_ref, out_ref, scratch):
    s = scratch
    gx, gy, *_ = place()
    meet([gy_peer(d) for d in range(1, GY)])
    core = lax.dot_general(
        bt_ref[...], f2_ref[...], (((1,), (0,)), ((), ())), precision=precise, preferred_element_type=jnp.float32
    )
    for u in range(GY):
        s["cs"][u, 0:3] = core[3 * u : 3 * (u + 1)]
        s["cs"][u, 3:8] = jnp.zeros((5, 128), jnp.float32)
    copies = []
    for d in range(1, GY):
        peer = gy_peer(d)
        copy = remote(s["cs"].at[peer[1]], s["rc"].at[gy], s["bs"].at[d - 1], s["br"].at[d - 1], peer)
        copy.start()
        copies.append(copy)
    s["rc"][gy] = s["cs"][gy]
    for copy in copies:
        copy.wait_recv()
    wide = jnp.concatenate([s["rc"][u][:, :COLS_TWO] for u in range(GY)], axis=1)
    for a in range(6):
        out_ref[a] = wide[0:3, COLS * a : COLS * (a + 1)]
    for copy in copies:
        copy.wait_send()


FIRST = REDUCE | dict(
    xs=pltpu.VMEM((GX, 32, COLS), jnp.float32), fib=pltpu.VMEM((GX, 32, COLS), jnp.float32),
    **{"as": DMA((15,)), "ar": DMA((15,))},
)
SECOND = REDUCE | dict(
    ss=pltpu.VMEM((GX, 8, COLS), jnp.float32), rs=pltpu.VMEM((GX, 8, COLS), jnp.float32),
    st=pltpu.VMEM((GY, GX, 128), jnp.float32), f2=pltpu.VMEM((GY, GX, 128), jnp.float32),
    bs=DMA((31,)), br=DMA((31,)), **{"as": DMA((15,)), "ar": DMA((15,))},
)
THIRD = dict(
    cs=pltpu.VMEM((GY, 8, 128), jnp.float32), rc=pltpu.VMEM((GY, 8, 128), jnp.float32),
    bs=DMA((31,)), br=DMA((31,)),
)

VMEM = pl.BlockSpec(memory_space=pltpu.VMEM)


def exchange(kernel, name, ident, outs, scratch):
    def body(*refs):
        count = len(refs) - 1
        kernel(*refs[:count], refs[count])

    def call(*args):
        single = len(outs) == 1
        shapes = [jax.ShapeDtypeStruct(o, jnp.float32) for o in outs]
        return pl.pallas_call(
            body,
            out_shape=shapes[0] if single else shapes,
            in_specs=[VMEM] * len(args),
            out_specs=VMEM if single else [VMEM] * len(outs),
            scratch_shapes=[scratch],
            compiler_params=pltpu.CompilerParams(
                collective_id=ident, has_side_effects=True, vmem_limit_bytes=32 * 1024 * 1024
            ),
            name=name,
        )(*args)

    return call


def normalize(images, cross_gram):
    factor = jnp.linalg.cholesky(cross_gram)
    return lax.linalg.triangular_solve(
        factor, images, left_side=False, lower=True, transpose_a=True
    )


def refine_whole(gram_full, initial):
    vectors = initial
    for sweep_index in range(ITERS):
        images = jnp.dot(gram_full, vectors, precision=precise)
        vectors = normalize(images, jnp.dot(images.T, images, precision=precise))
    return vectors


def whole(blocks, scale):
    b = {}
    for n, (p, q) in enumerate(BLOCKS):
        block = blocks[128 * n : 128 * (n + 1)] * scale
        b[p, q] = block
        if p != q:
            b[q, p] = block.T
    return jnp.concatenate([jnp.concatenate([b[p, q] for q in range(4)], axis=1) for p in range(4)], axis=0)


def body(snapshot, start_one, start_two):
    fibers, blocks = exchange(first_kernel, "first", 0, [(I1, COLS), (GROWS, 128)], FIRST)(snapshot)
    basis_one = refine_whole(whole(blocks, 1.0 / (I2 * COLS)), start_one)
    fibers_two, blocks = exchange(second_kernel, "second", 1, [(I2, 128), (GROWS, 128)], SECOND)(basis_one.T, fibers)
    basis_two = refine_whole(whole(blocks, 1.0 / (RANK * COLS)), start_two)
    core_tensor = exchange(third_kernel, "third", 2, [(6, 3, COLS)], THIRD)(basis_two.T, fibers_two)
    return (basis_one, basis_two, core_tensor)


def solution(mesh):
    in_specs = (P("gx", "gy", None), P(), P())
    out_specs = (P(), P(), P("gx", "gy", None))
    return jax.shard_map(body, mesh=mesh, in_specs=in_specs, out_specs=out_specs, check_vma=False)
```

```python
import functools

import jax
import jax.numpy as jnp
from jax import lax
from jax.experimental import pallas as pl
from jax.experimental.pallas import tpu as pltpu
from jax.sharding import PartitionSpec as P

I1 = 512
I2 = 512
COLS = 384
RANK = 96
ITERS = 6
GX = 16
GY = 32
NX = 4
NY = 4
NZ = 16
BLOCKS = [(p, q) for p in range(4) for q in range(p, 4)]
GROWS = 128 * len(BLOCKS)
HALF = GROWS // 2
PIECE = HALF // 16
OWNERS = (0, 3, 6, 9, 12)
COLS_TWO = 6 * COLS // GY

MESH = pl.DeviceIdType.MESH
precise = lax.Precision.HIGHEST


def place():
    gx = lax.axis_index("gx")
    gy = lax.axis_index("gy")
    x, z_lo = lax.div(gx, 4), lax.rem(gx, 4)
    z_hi = lax.div(gy, 8)
    y = lax.rem(lax.div(gy, 2), 4)
    core = lax.rem(gy, 2)
    return gx, gy, x, y, z_hi, z_lo, core


def remote(src, dst, send, recv, target):
    return pltpu.make_async_remote_copy(
        src_ref=src, dst_ref=dst, send_sem=send, recv_sem=recv, device_id=target, device_id_type=MESH
    )


def gx_peer(d):
    gx, gy = place()[:2]
    return (lax.rem(gx + d, GX), gy)


def gy_peer(d):
    gx, gy = place()[:2]
    return (gx, lax.rem(gy + d, GY))


def sibling():
    gx, gy, *_, core = place()
    return (gx, gy + 1 - 2 * core)


def xy_peer(dx, dy):
    gx, gy, x, y, z_hi, z_lo, core = place()
    px, py = lax.rem(x + dx, NX), lax.rem(y + dy, NY)
    return (px * 4 + z_lo, z_hi * 8 + py * 2 + core), px * 4 + py


def z_peer(z):
    gx, gy, x, y, z_hi, z_lo, core = place()
    return (x * 4 + z % 4, (z // 4) * 8 + y * 2 + core)


def zz_peer(dh, dl):
    gx, gy, x, y, z_hi, z_lo, core = place()
    return (x * 4 + lax.rem(z_lo + dl, 4), lax.rem(z_hi + dh, 4) * 8 + y * 2 + core)


def meet(peers):
    barrier = pltpu.get_barrier_semaphore()
    for peer in peers:
        pl.semaphore_signal(barrier, inc=1, device_id=peer, device_id_type=MESH)
    pl.semaphore_wait(barrier, len(peers))


XY = [(dx, dy) for dx in range(NX) for dy in range(NY) if (dx, dy) != (0, 0)]


def all_reduce(gp, total, s):
    gx, gy, x, y, z_hi, z_lo, core = place()
    z = z_hi * 4 + z_lo
    mine = pl.multiple_of(core * HALF, 8)
    other = pl.multiple_of((1 - core) * HALF, 8)
    done = []
    copy = remote(gp.at[pl.ds(other, HALF)], s["rc"], s["c1s"], s["c1r"], sibling())
    copy.start()
    copy.wait_recv()
    done.append(copy)
    s["h"][...] = gp[pl.ds(mine, HALF)] + s["rc"][...]
    copies = []
    for o, (dx, dy) in enumerate(XY):
        peer, q = xy_peer(dx, dy)
        copy = remote(
            s["h"].at[pl.ds(pl.multiple_of(q * PIECE, 8), PIECE)],
            s["rxy"].at[o], s["x1s"].at[o], s["x1r"].at[o], peer,
        )
        copy.start()
        copies.append(copy)
    me = x * 4 + y
    acc = s["h"][pl.ds(pl.multiple_of(me * PIECE, 8), PIECE)]
    for o, copy in enumerate(copies):
        copy.wait_recv()
        acc = acc + s["rxy"][o]
    s["acc"][...] = acc
    done += copies
    def rows(w):
        return pl.ds(8 * w, 8)

    def to_owner(w):
        zw = OWNERS[w]
        return remote(s["acc"].at[rows(w)], s["rz"].at[z], s["z1s"].at[w], s["z1r"].at[z], z_peer(zw))

    def from_owner(w, target):
        return remote(s["agz"].at[rows(w)], s["agz"].at[rows(w)], s["z2s"].at[target], s["z2r"].at[w], z_peer(target))

    for w, zw in enumerate(OWNERS):
        @pl.when(z != zw)
        def _(w=w):
            to_owner(w).start()
    for w, zw in enumerate(OWNERS):
        @pl.when(z == zw)
        def _(w=w, zw=zw):
            part = s["acc"][rows(w)]
            others = [i for i in range(NZ) if i != zw]
            for i in others:
                remote(s["acc"].at[rows(w)], s["rz"].at[i], s["z1s"].at[w], s["z1r"].at[i], z_peer(i)).wait_recv()
                part = part + s["rz"][i]
            s["agz"][rows(w)] = part
            for i in others:
                from_owner(w, i).start()
    for w, zw in enumerate(OWNERS):
        @pl.when(z != zw)
        def _(w=w, zw=zw):
            from_owner(w, zw).wait_recv()
    own = pl.ds(pl.multiple_of(mine + me * PIECE, 8), PIECE)
    copies = []
    for o, (dx, dy) in enumerate(XY):
        peer, q = xy_peer(dx, dy)
        copy = remote(s["agz"], total.at[own], s["x2s"].at[o], s["x2r"].at[o], peer)
        copy.start()
        copies.append(copy)
    total[own] = s["agz"][...]
    for copy in copies:
        copy.wait_recv()
    done += copies
    copy = remote(total.at[pl.ds(mine, HALF)], total.at[pl.ds(mine, HALF)], s["c2s"], s["c2r"], sibling())
    copy.start()
    copy.wait_recv()
    done.append(copy)
    for copy in done:
        copy.wait_send()
    for w, zw in enumerate(OWNERS):
        @pl.when(z != zw)
        def _(w=w):
            to_owner(w).wait_send()

        @pl.when(z == zw)
        def _(w=w, zw=zw):
            for i in range(NZ):
                if i != zw:
                    from_owner(w, i).wait_send()


DMA = pltpu.SemaphoreType.DMA
REDUCE = dict(
    gp=pltpu.VMEM((GROWS, 128), jnp.float32),
    total=pltpu.VMEM((GROWS, 128), jnp.float32),
    rc=pltpu.VMEM((HALF, 128), jnp.float32),
    h=pltpu.VMEM((HALF, 128), jnp.float32),
    rxy=pltpu.VMEM((15, PIECE, 128), jnp.float32),
    acc=pltpu.VMEM((PIECE, 128), jnp.float32),
    rz=pltpu.VMEM((NZ, 8, 128), jnp.float32),
    agz=pltpu.VMEM((PIECE, 128), jnp.float32),
    c1s=DMA, c1r=DMA, c2s=DMA, c2r=DMA,
    x1s=DMA((15,)), x1r=DMA((15,)), x2s=DMA((15,)), x2r=DMA((15,)),
    z1s=DMA((5,)), z1r=DMA((NZ,)), z2s=DMA((NZ,)), z2r=DMA((5,)),
)


def gram_blocks(flat, gp):
    n = 0
    for p in range(4):
        strip = lax.dot_general(
            flat[128 * p : 128 * (p + 1)], flat[128 * p :], (((1,), (1,)), ((), ())),
            precision=precise, preferred_element_type=jnp.float32,
        )
        for q in range(4 - p):
            gp[128 * n : 128 * (n + 1)] = strip[:, 128 * q : 128 * (q + 1)]
            n += 1


def reduce_peers():
    peers = [xy_peer(dx, dy)[0] for dx in range(1, NX) for dy in range(1, NY)]
    return peers + [zz_peer(a, b) for a in range(1, 4) for b in range(1, 4)]


def first_kernel(x_ref, fib_ref, g_ref, scratch):
    s = scratch
    gx, gy, *_ = place()
    meet([gx_peer(d) for d in range(1, GX)] + [gy_peer(d) for d in range(1, GY)] + reduce_peers())
    for j in range(GX):
        s["xs"][j] = x_ref[:, j, :]
    copies = []
    for d in range(1, GX):
        peer = gx_peer(d)
        copy = remote(s["xs"].at[peer[0]], s["fib"].at[gx], s["as"].at[d - 1], s["ar"].at[d - 1], peer)
        copy.start()
        copies.append(copy)
    s["fib"][gx] = s["xs"][gx]
    for copy in copies:
        copy.wait_recv()
    flat = s["fib"][...].reshape(I1, COLS)
    fib_ref[...] = flat
    gram_blocks(flat, s["gp"])
    all_reduce(s["gp"], s["total"], s)
    g_ref[...] = s["total"][...]
    for copy in copies:
        copy.wait_send()


def second_kernel(bt_ref, fib_ref, f2_ref, g_ref, scratch):
    s = scratch
    gx, gy, *_ = place()
    meet([gx_peer(d) for d in range(1, GX)] + [gy_peer(d) for d in range(1, GY)] + reduce_peers())
    shrunk = lax.dot_general(
        bt_ref[...], fib_ref[...], (((1,), (0,)), ((), ())), precision=precise, preferred_element_type=jnp.float32
    )
    for g in range(GX):
        s["ss"][g, 0:6] = shrunk[6 * g : 6 * (g + 1)]
        s["ss"][g, 6:8] = jnp.zeros((2, COLS), jnp.float32)
    copies = []
    for d in range(1, GX):
        peer = gx_peer(d)
        copy = remote(s["ss"].at[peer[0]], s["rs"].at[gx], s["as"].at[d - 1], s["ar"].at[d - 1], peer)
        copy.start()
        copies.append(copy)
    s["rs"][gx] = s["ss"][gx]
    for copy in copies:
        copy.wait_recv()
    wide = jnp.concatenate([s["rs"][:, a, :] for a in range(6)], axis=1)
    pad = jnp.zeros((GX, 128 - COLS_TWO), jnp.float32)
    for u in range(GY):
        s["st"][u] = jnp.concatenate([wide[:, COLS_TWO * u : COLS_TWO * (u + 1)], pad], axis=1)
    seconds = []
    for d in range(1, GY):
        peer = gy_peer(d)
        copy = remote(s["st"].at[peer[1]], s["f2"].at[gy], s["bs"].at[d - 1], s["br"].at[d - 1], peer)
        copy.start()
        seconds.append(copy)
    s["f2"][gy] = s["st"][gy]
    for copy in seconds:
        copy.wait_recv()
    flat = s["f2"][...].reshape(I2, 128)
    f2_ref[...] = flat
    gram_blocks(flat, s["gp"])
    all_reduce(s["gp"], s["total"], s)
    g_ref[...] = s["total"][...]
    for copy in copies + seconds:
        copy.wait_send()


def third_kernel(bt_ref, f2_ref, out_ref, scratch):
    s = scratch
    gx, gy, *_ = place()
    meet([gy_peer(d) for d in range(1, GY)])
    core = lax.dot_general(
        bt_ref[...], f2_ref[...], (((1,), (0,)), ((), ())), precision=precise, preferred_element_type=jnp.float32
    )
    for u in range(GY):
        s["cs"][u, 0:3] = core[3 * u : 3 * (u + 1)]
        s["cs"][u, 3:8] = jnp.zeros((5, 128), jnp.float32)
    copies = []
    for d in range(1, GY):
        peer = gy_peer(d)
        copy = remote(s["cs"].at[peer[1]], s["rc"].at[gy], s["bs"].at[d - 1], s["br"].at[d - 1], peer)
        copy.start()
        copies.append(copy)
    s["rc"][gy] = s["cs"][gy]
    for copy in copies:
        copy.wait_recv()
    wide = jnp.concatenate([s["rc"][u][:, :COLS_TWO] for u in range(GY)], axis=1)
    for a in range(6):
        out_ref[a] = wide[0:3, COLS * a : COLS * (a + 1)]
    for copy in copies:
        copy.wait_send()


FIRST = REDUCE | dict(
    xs=pltpu.VMEM((GX, 32, COLS), jnp.float32), fib=pltpu.VMEM((GX, 32, COLS), jnp.float32),
    **{"as": DMA((15,)), "ar": DMA((15,))},
)
SECOND = REDUCE | dict(
    ss=pltpu.VMEM((GX, 8, COLS), jnp.float32), rs=pltpu.VMEM((GX, 8, COLS), jnp.float32),
    st=pltpu.VMEM((GY, GX, 128), jnp.float32), f2=pltpu.VMEM((GY, GX, 128), jnp.float32),
    bs=DMA((31,)), br=DMA((31,)), **{"as": DMA((15,)), "ar": DMA((15,))},
)
THIRD = dict(
    cs=pltpu.VMEM((GY, 8, 128), jnp.float32), rc=pltpu.VMEM((GY, 8, 128), jnp.float32),
    bs=DMA((31,)), br=DMA((31,)),
)

VMEM = pl.BlockSpec(memory_space=pltpu.VMEM)


def exchange(kernel, name, ident, outs, scratch):
    def body(*refs):
        count = len(refs) - 1
        kernel(*refs[:count], refs[count])

    def call(*args):
        single = len(outs) == 1
        shapes = [jax.ShapeDtypeStruct(o, jnp.float32) for o in outs]
        return pl.pallas_call(
            body,
            out_shape=shapes[0] if single else shapes,
            in_specs=[VMEM] * len(args),
            out_specs=VMEM if single else [VMEM] * len(outs),
            scratch_shapes=[scratch],
            compiler_params=pltpu.CompilerParams(
                collective_id=ident, has_side_effects=True, vmem_limit_bytes=32 * 1024 * 1024
            ),
            name=name,
        )(*args)

    return call


def dot(a, b, dims=((1,), (0,))):
    return lax.dot_general(a, b, (dims, ((), ())), precision=precise, preferred_element_type=jnp.float32)


def inverse_factor(c):
    lane = lax.broadcasted_iota(jnp.int32, (8, 128), 1)
    row = lax.broadcasted_iota(jnp.int32, (8, 128), 0)
    tiles = [c[8 * i : 8 * (i + 1)] for i in range(RANK // 8)]
    result = []

    def spread_lane(tile, n):
        return jnp.broadcast_to(tile[:, n : n + 1], (8, 128))

    def spread_row(tile, n):
        return jnp.broadcast_to(tile[n : n + 1, :], (8, 128))

    for k in range(RANK // 8):
        lo = 8 * k
        inside = (lane >= lo) & (lane < lo + 8)
        columns = [[spread_lane(tiles[i], lo + t) for t in range(8)] for i in range(k, RANK // 8)]
        d = [[spread_row(columns[0][t], s) for t in range(s + 1)] for s in range(8)]
        unit = jnp.where(inside, jnp.where(lane - lo == row, 1.0, 0.0), tiles[k])
        p = [spread_row(unit, s) for s in range(8)]
        rd = [None] * 8
        m = [[None] * 8 for _ in range(8)]
        for t in range(8):
            rd[t] = 1.0 / d[t][t]
            for s in range(t + 1, 8):
                m[s][t] = d[s][t] * rd[t]
                for u in range(t + 1, s + 1):
                    d[s][u] = d[s][u] - m[s][t] * d[u][t]
                p[s] = p[s] - m[s][t] * p[t]
        rows = p[0] * lax.rsqrt(d[0][0])
        for s in range(1, 8):
            rows = jnp.where(row == s, p[s] * lax.rsqrt(d[s][s]), rows)
        result.append(jnp.where(lane < lo + 8, rows, 0.0))
        if k + 1 == RANK // 8:
            break
        q = [p[t] * rd[t] for t in range(8)]
        for s in range(7, 0, -1):
            for t in range(s):
                q[t] = q[t] - m[s][t] * q[s]
        for i in range(k + 1, RANK // 8):
            col = columns[i - k]
            new = jnp.where(inside, 0.0, tiles[i])
            for t in range(8):
                new = new - col[t] * q[t]
            tiles[i] = new
    return jnp.concatenate(result, axis=0)


def refine_kernel(scale, blocks_ref, start_ref, out_ref, g_ref):
    for n, (p, q) in enumerate(BLOCKS):
        block = blocks_ref[128 * n : 128 * (n + 1)] * scale
        g_ref[128 * p : 128 * (p + 1), 128 * q : 128 * (q + 1)] = block
        if p != q:
            g_ref[128 * q : 128 * (q + 1), 128 * p : 128 * (p + 1)] = block.T
    pad = jnp.zeros((128 - RANK, 512), jnp.float32)

    def factor(images):
        full = jnp.concatenate([images, pad], axis=0)
        return inverse_factor(dot(images, full, ((1,), (1,))))

    def sweep(_, images):
        ahead = dot(images, g_ref[...])
        return dot(factor(images), jnp.concatenate([ahead, pad], axis=0))

    images = dot(start_ref[...], g_ref[...])
    images = lax.fori_loop(0, ITERS - 1, sweep, images)
    out_ref[...] = dot(factor(images), jnp.concatenate([images, pad], axis=0))


def refine(blocks, start_t, scale, name):
    vmem = pl.BlockSpec(memory_space=pltpu.VMEM)
    return pl.pallas_call(
        functools.partial(refine_kernel, scale),
        out_shape=jax.ShapeDtypeStruct((RANK, 512), jnp.float32),
        in_specs=[vmem] * 2,
        out_specs=vmem,
        scratch_shapes=[pltpu.VMEM((512, 512), jnp.float32)],
        compiler_params=pltpu.CompilerParams(vmem_limit_bytes=32 * 1024 * 1024),
        name=name,
    )(blocks, start_t)


def body(snapshot, start_one, start_two):
    fibers, blocks = exchange(first_kernel, "first", 0, [(I1, COLS), (GROWS, 128)], FIRST)(snapshot)
    basis_one = refine(blocks, start_one.T, 1.0 / (I2 * COLS), "refine_one")
    fibers_two, blocks = exchange(second_kernel, "second", 1, [(I2, 128), (GROWS, 128)], SECOND)(basis_one, fibers)
    basis_two = refine(blocks, start_two.T, 1.0 / (RANK * COLS), "refine_two")
    core_tensor = exchange(third_kernel, "third", 2, [(6, 3, COLS)], THIRD)(basis_two, fibers_two)
    return (basis_one.T, basis_two.T, core_tensor)


def solution(mesh):
    in_specs = (P("gx", "gy", None), P(), P())
    out_specs = (P(), P(), P("gx", "gy", None))
    return jax.shard_map(body, mesh=mesh, in_specs=in_specs, out_specs=out_specs, check_vma=False)
```

```python
import functools

import jax
import jax.numpy as jnp
from jax import lax
from jax.experimental import pallas as pl
from jax.experimental.pallas import tpu as pltpu
from jax.sharding import PartitionSpec as P

I1 = 512
I2 = 512
COLS = 384
RANK = 96
ITERS = 6
GX = 16
GY = 32
NX = 4
NY = 4
BLOCKS = [(p, q) for p in range(4) for q in range(p, 4)]
GROWS = 128 * len(BLOCKS)
HALF = GROWS // 2
PIECE = HALF // 16
QUARTER = PIECE // 4

MESH = pl.DeviceIdType.MESH
precise = lax.Precision.HIGHEST


def place():
    gx = lax.axis_index("gx")
    gy = lax.axis_index("gy")
    x, z_lo = lax.div(gx, 4), lax.rem(gx, 4)
    z_hi = lax.div(gy, 8)
    y = lax.rem(lax.div(gy, 2), 4)
    core = lax.rem(gy, 2)
    return gx, gy, x, y, z_hi, z_lo, core


def remote(src, dst, send, recv, target):
    return pltpu.make_async_remote_copy(
        src_ref=src, dst_ref=dst, send_sem=send, recv_sem=recv, device_id=target, device_id_type=MESH
    )


def gx_peer(d):
    gx, gy = place()[:2]
    return (lax.rem(gx + d, GX), gy)


def gy_peer(d):
    gx, gy = place()[:2]
    return (gx, lax.bitwise_xor(gy, d))


def sibling():
    gx, gy, *_, core = place()
    return (gx, gy + 1 - 2 * core)


def xy_peer(dx, dy):
    gx, gy, x, y, z_hi, z_lo, core = place()
    px, py = lax.rem(x + dx, NX), lax.rem(y + dy, NY)
    return (px * 4 + z_lo, z_hi * 8 + py * 2 + core), px * 4 + py


def z_lo_peer(d):
    gx, gy, x, y, z_hi, z_lo, core = place()
    other = lax.rem(z_lo + d, 4)
    return (x * 4 + other, gy), other


def z_hi_peer(d):
    gx, gy, x, y, z_hi, z_lo, core = place()
    return (gx, lax.rem(z_hi + d, 4) * 8 + y * 2 + core)


def meet(peers):
    barrier = pltpu.get_barrier_semaphore()
    for peer in peers:
        pl.semaphore_signal(barrier, inc=1, device_id=peer, device_id_type=MESH)
    pl.semaphore_wait(barrier, len(peers))


XY = [(dx, dy) for dx in range(NX) for dy in range(NY) if (dx, dy) != (0, 0)]


def all_reduce(gp, total, s):
    gx, gy, x, y, z_hi, z_lo, core = place()
    mine = pl.multiple_of(core * HALF, 8)
    other = pl.multiple_of((1 - core) * HALF, 8)
    done = []
    copy = remote(gp.at[pl.ds(other, HALF)], s["rc"], s["c1s"], s["c1r"], sibling())
    copy.start()
    copy.wait_recv()
    done.append(copy)
    s["h"][...] = gp[pl.ds(mine, HALF)] + s["rc"][...]
    copies = []
    for o, (dx, dy) in enumerate(XY):
        peer, q = xy_peer(dx, dy)
        copy = remote(
            s["h"].at[pl.ds(pl.multiple_of(q * PIECE, 8), PIECE)],
            s["rxy"].at[o], s["x1s"].at[o], s["x1r"].at[o], peer,
        )
        copy.start()
        copies.append(copy)
    me = x * 4 + y
    acc = s["h"][pl.ds(pl.multiple_of(me * PIECE, 8), PIECE)]
    for o, copy in enumerate(copies):
        copy.wait_recv()
        acc = acc + s["rxy"][o]
    done += copies
    for i in range(4):
        s["za"][i] = acc[QUARTER * i : QUARTER * (i + 1)]
    copies = []
    for d in range(1, 4):
        peer, other = z_lo_peer(d)
        copy = remote(s["za"].at[other], s["rzl"].at[d - 1], s["z1s"].at[d - 1], s["z1r"].at[d - 1], peer)
        copy.start()
        copies.append(copy)
    part = s["za"][z_lo]
    for d, copy in enumerate(copies):
        copy.wait_recv()
        part = part + s["rzl"][d]
    done += copies
    s["zh"][z_hi] = part
    copies = []
    for d in range(1, 4):
        copy = remote(s["zh"].at[z_hi], s["zh"].at[z_hi], s["z2s"].at[d - 1], s["z2r"].at[d - 1], z_hi_peer(d))
        copy.start()
        copies.append(copy)
    for copy in copies:
        copy.wait_recv()
    done += copies
    s["zl"][z_lo] = (s["zh"][0] + s["zh"][1]) + (s["zh"][2] + s["zh"][3])
    copies = []
    for d in range(1, 4):
        peer, _ = z_lo_peer(d)
        copy = remote(s["zl"].at[z_lo], s["zl"].at[z_lo], s["z3s"].at[d - 1], s["z3r"].at[d - 1], peer)
        copy.start()
        copies.append(copy)
    for copy in copies:
        copy.wait_recv()
    done += copies
    s["agz"][...] = jnp.concatenate([s["zl"][i] for i in range(4)], axis=0)
    own = pl.ds(pl.multiple_of(mine + me * PIECE, 8), PIECE)
    copies = []
    for o, (dx, dy) in enumerate(XY):
        peer, q = xy_peer(dx, dy)
        copy = remote(s["agz"], total.at[own], s["x2s"].at[o], s["x2r"].at[o], peer)
        copy.start()
        copies.append(copy)
    total[own] = s["agz"][...]
    for copy in copies:
        copy.wait_recv()
    done += copies
    copy = remote(total.at[pl.ds(mine, HALF)], total.at[pl.ds(mine, HALF)], s["c2s"], s["c2r"], sibling())
    copy.start()
    copy.wait_recv()
    done.append(copy)
    for copy in done:
        copy.wait_send()


DMA = pltpu.SemaphoreType.DMA
REDUCE = dict(
    gp=pltpu.VMEM((GROWS, 128), jnp.float32),
    total=pltpu.VMEM((GROWS, 128), jnp.float32),
    rc=pltpu.VMEM((HALF, 128), jnp.float32),
    h=pltpu.VMEM((HALF, 128), jnp.float32),
    rxy=pltpu.VMEM((15, PIECE, 128), jnp.float32),
    za=pltpu.VMEM((4, QUARTER, 128), jnp.float32),
    rzl=pltpu.VMEM((3, QUARTER, 128), jnp.float32),
    zh=pltpu.VMEM((4, QUARTER, 128), jnp.float32),
    zl=pltpu.VMEM((4, QUARTER, 128), jnp.float32),
    agz=pltpu.VMEM((PIECE, 128), jnp.float32),
    c1s=DMA, c1r=DMA, c2s=DMA, c2r=DMA,
    x1s=DMA((15,)), x1r=DMA((15,)), x2s=DMA((15,)), x2r=DMA((15,)),
    z1s=DMA((3,)), z1r=DMA((3,)), z2s=DMA((3,)), z2r=DMA((3,)), z3s=DMA((3,)), z3r=DMA((3,)),
)


def gram_blocks(flat, gp):
    n = 0
    for p in range(4):
        strip = lax.dot_general(
            flat[128 * p : 128 * (p + 1)], flat[128 * p :], (((1,), (1,)), ((), ())),
            precision=precise, preferred_element_type=jnp.float32,
        )
        for q in range(4 - p):
            gp[128 * n : 128 * (n + 1)] = strip[:, 128 * q : 128 * (q + 1)]
            n += 1


def swap_granules(tiles):
    lane = lax.broadcasted_iota(jnp.int32, tiles[0].shape, 1)
    tiles = list(tiles)
    for bit in range(4):
        shift = 8 << bit
        low = lax.bitwise_and(lane, shift) == 0
        for j in range(16):
            if not j >> bit & 1:
                k = j | 1 << bit
                a, b = tiles[j], tiles[k]
                tiles[j] = jnp.where(low, a, pltpu.roll(b, shift, 1))
                tiles[k] = jnp.where(low, pltpu.roll(a, 128 - shift, 1), b)
    return tiles


def plane_peers():
    return [xy_peer(dx, dy)[0] for dx in range(1, NX) for dy in range(1, NY)]


def gather_one(x_ref, s):
    gx, gy, *_ = place()
    copies = []
    for half in range(2):
        for i in range(2 * half, 2 * half + 2):
            rows = slice(8 * i, 8 * (i + 1))
            for c in range(3):
                lanes = slice(128 * c, 128 * (c + 1))
                for g, tile in enumerate(swap_granules([x_ref[rows, j, lanes] for j in range(16)])):
                    s["xs"][g, rows, lanes] = tile
        rows = pl.ds(16 * half, 16)
        for d in range(1, GX):
            peer = gx_peer(d)
            copy = remote(
                s["xs"].at[peer[0], rows], s["fib"].at[gx, rows],
                s["as"].at[half, d - 1], s["ar"].at[half, d - 1], peer,
            )
            copy.start()
            copies.append(copy)
    s["fib"][gx] = s["xs"][gx]
    for copy in copies:
        copy.wait_recv()
    return copies


def gather_two(basis, fibers, s):
    gx, gy, *_ = place()
    shrunk = dot(basis, fibers)
    for u in range(GY):
        s["st"][u] = shrunk[3 * u : 3 * (u + 1)]
    copies = []
    for d in range(1, GY):
        peer = gy_peer(d)
        copy = remote(s["st"].at[peer[1]], s["f2"].at[gy], s["bs"].at[d - 1], s["br"].at[d - 1], peer)
        copy.start()
        copies.append(copy)
    s["f2"][gy] = s["st"][gy]
    for copy in copies:
        copy.wait_recv()
    tiles = [s["f2"][:, a, 128 * c : 128 * (c + 1)] for a in range(3) for c in range(3)]
    tiles += [jnp.zeros((GY, 128), jnp.float32)] * 7
    return jnp.concatenate(swap_granules(tiles), axis=0), copies


def spread_core(basis, columns, out_ref, s):
    gx, gy, *_ = place()
    row, half = lax.div(gy, 2), lax.rem(gy, 2)
    core = dot(basis, columns)
    for u in range(GY):
        s["cs"][u] = core[3 * u : 3 * (u + 1)]

    def copy(d):
        u = lax.bitwise_xor(gy, d)
        return remote(s["cs"].at[u], s["ro"].at[gx, half], s["ks"].at[d], s["kr"].at[gx, half], (row, u))

    @pl.when(row != gx)
    def _():
        copy(0).start()

    @pl.when(row == gx)
    def _():
        s["ro"][gx, half] = s["cs"][gy]

    for d in range(1, GY):
        copy(d).start()

    def arrival(k, h):
        source = lax.rem(gx + k, GX)
        return remote(s["cs"].at[0], s["ro"].at[source, h], s["ks"].at[0], s["kr"].at[source, h], (source, 2 * gx + h))

    for h in range(2):
        @pl.when(2 * gx + h != gy)
        def _(h=h):
            arrival(0, h).wait_recv()
        for k in range(1, GX):
            arrival(k, h).wait_recv()
    for h in range(2):
        tiles = swap_granules([s["ro"][g, h] for g in range(GX)])
        for a in range(3):
            for c in range(3):
                out_ref[3 * h + a, :, 128 * c : 128 * (c + 1)] = tiles[3 * a + c]

    @pl.when(row != gx)
    def _():
        copy(0).wait_send()

    for d in range(1, GY):
        copy(d).wait_send()


def first_kernel(x_ref, fib_ref, g_ref, s):
    meet([gx_peer(d) for d in range(1, GX)] + [gy_peer(d) for d in range(1, GY)] + plane_peers())
    copies = gather_one(x_ref, s)
    flat = s["fib"][...].reshape(I1, COLS)
    fib_ref[...] = flat
    gram_blocks(flat, s["gp"])
    all_reduce(s["gp"], s["total"], s)
    g_ref[...] = s["total"][...]
    for copy in copies:
        copy.wait_send()


def second_kernel(basis_ref, fib_ref, f2_ref, g_ref, s):
    meet([gx_peer(d) for d in range(1, GX)] + [gy_peer(d) for d in range(1, GY)] + plane_peers())
    flat, copies = gather_two(basis_ref[...], fib_ref[...], s)
    f2_ref[...] = flat
    gram_blocks(flat, s["gp"])
    all_reduce(s["gp"], s["total"], s)
    g_ref[...] = s["total"][...]
    for copy in copies:
        copy.wait_send()


def third_kernel(basis_ref, f2_ref, out_ref, s):
    gx, gy, *_ = place()
    barrier = pltpu.get_barrier_semaphore()
    for h in range(2):
        @pl.when(2 * gx + h != gy)
        def _(h=h):
            pl.semaphore_signal(barrier, inc=1, device_id=(gx, 2 * gx + h), device_id_type=MESH)
        for k in range(1, GX):
            pl.semaphore_signal(barrier, inc=1, device_id=(lax.rem(gx + k, GX), 2 * gx + h), device_id_type=MESH)

    @pl.when(lax.div(gy, 2) == gx)
    def _():
        pl.semaphore_wait(barrier, 31)

    @pl.when(lax.div(gy, 2) != gx)
    def _():
        pl.semaphore_wait(barrier, 32)

    spread_core(basis_ref[...], f2_ref[...], out_ref, s)


FIRST = REDUCE | dict(
    xs=pltpu.VMEM((GX, 32, COLS), jnp.float32), fib=pltpu.VMEM((GX, 32, COLS), jnp.float32),
    **{"as": DMA((2, 15)), "ar": DMA((2, 15))},
)
SECOND = REDUCE | dict(
    st=pltpu.VMEM((GY, 3, COLS), jnp.float32), f2=pltpu.VMEM((GY, 3, COLS), jnp.float32),
    bs=DMA((31,)), br=DMA((31,)),
)
THIRD = dict(
    cs=pltpu.VMEM((GY, 3, 128), jnp.float32), ro=pltpu.VMEM((GX, 2, 3, 128), jnp.float32),
    ks=DMA((32,)), kr=DMA((GX, 2)),
)

VMEM = pl.BlockSpec(memory_space=pltpu.VMEM)


def exchange(kernel, name, ident, outs, scratch):
    def body(*refs):
        count = len(refs) - 1
        kernel(*refs[:count], refs[count])

    def call(*args):
        single = len(outs) == 1
        shapes = [jax.ShapeDtypeStruct(o, jnp.float32) for o in outs]
        return pl.pallas_call(
            body,
            out_shape=shapes[0] if single else shapes,
            in_specs=[VMEM] * len(args),
            out_specs=VMEM if single else [VMEM] * len(outs),
            scratch_shapes=[scratch],
            compiler_params=pltpu.CompilerParams(
                collective_id=ident, has_side_effects=True, vmem_limit_bytes=32 * 1024 * 1024
            ),
            name=name,
        )(*args)

    return call


def dot(a, b, dims=((1,), (0,))):
    return lax.dot_general(a, b, (dims, ((), ())), precision=precise, preferred_element_type=jnp.float32)


def inverse_factor(c):
    lane = lax.broadcasted_iota(jnp.int32, (8, 128), 1)
    row = lax.broadcasted_iota(jnp.int32, (8, 128), 0)
    tiles = [c[8 * i : 8 * (i + 1)] for i in range(RANK // 8)]
    result = []

    def spread_lane(tile, n):
        return jnp.broadcast_to(tile[:, n : n + 1], (8, 128))

    def spread_row(tile, n):
        return jnp.broadcast_to(tile[n : n + 1, :], (8, 128))

    for k in range(RANK // 8):
        lo = 8 * k
        inside = (lane >= lo) & (lane < lo + 8)
        columns = [[spread_lane(tiles[i], lo + t) for t in range(8)] for i in range(k, min(k + 2 + 1, RANK // 8))]
        d = [[spread_row(columns[0][t], s) for t in range(s + 1)] for s in range(8)]
        unit = jnp.where(inside, jnp.where(lane - lo == row, 1.0, 0.0), tiles[k])
        p = [spread_row(unit, s) for s in range(8)]
        rd = [None] * 8
        m = [[None] * 8 for _ in range(8)]
        for t in range(8):
            rd[t] = 1.0 / d[t][t]
            for s in range(t + 1, 8):
                m[s][t] = d[s][t] * rd[t]
                for u in range(t + 1, s + 1):
                    d[s][u] = d[s][u] - m[s][t] * d[u][t]
                p[s] = p[s] - m[s][t] * p[t]
        rows = p[0] * lax.rsqrt(d[0][0])
        for s in range(1, 8):
            rows = jnp.where(row == s, p[s] * lax.rsqrt(d[s][s]), rows)
        result.append(jnp.where(lane < lo + 8, rows, 0.0))
        if k + 1 == RANK // 8:
            break
        q = [p[t] * rd[t] for t in range(8)]
        for s in range(7, 0, -1):
            for t in range(s):
                q[t] = q[t] - m[s][t] * q[s]
        near = min(k + 2, RANK // 8 - 1)
        if near + 1 < RANK // 8:
            picked = q[0]
            for t in range(1, 8):
                picked = jnp.where(row == t, q[t], picked)
            spread = [picked] if k == 0 else [jnp.zeros((lo, 128), jnp.float32), picked]
            spread = jnp.concatenate(spread + [jnp.zeros((120 - lo, 128), jnp.float32)], axis=0)
            far = jnp.concatenate(tiles[near + 1 :], axis=0)
            change = dot(far, spread)
        for i in range(k + 1, RANK // 8):
            new = jnp.where(inside, 0.0, tiles[i])
            if i <= near:
                col = columns[i - k]
                for t in range(8):
                    new = new - col[t] * q[t]
            else:
                at = 8 * (i - near - 1)
                new = new - change[at : at + 8]
            tiles[i] = new
    return jnp.concatenate(result, axis=0)


def refine_kernel(scale, blocks_ref, start_ref, out_ref, g_ref):
    for n, (p, q) in enumerate(BLOCKS):
        block = blocks_ref[128 * n : 128 * (n + 1)] * scale
        g_ref[128 * p : 128 * (p + 1), 128 * q : 128 * (q + 1)] = block
        if p != q:
            g_ref[128 * q : 128 * (q + 1), 128 * p : 128 * (p + 1)] = block.T
    pad = jnp.zeros((128 - RANK, 512), jnp.float32)

    def factor(images):
        full = jnp.concatenate([images, pad], axis=0)
        return inverse_factor(dot(images, full, ((1,), (1,))))

    def sweep(_, images):
        ahead = dot(images, g_ref[...])
        return dot(factor(images), jnp.concatenate([ahead, pad], axis=0))

    images = dot(start_ref[...], g_ref[...])
    images = lax.fori_loop(0, ITERS - 1, sweep, images)
    out_ref[...] = dot(factor(images), jnp.concatenate([images, pad], axis=0))


def refine(blocks, start_t, scale, name):
    vmem = pl.BlockSpec(memory_space=pltpu.VMEM)
    return pl.pallas_call(
        functools.partial(refine_kernel, scale),
        out_shape=jax.ShapeDtypeStruct((RANK, 512), jnp.float32),
        in_specs=[vmem] * 2,
        out_specs=vmem,
        scratch_shapes=[pltpu.VMEM((512, 512), jnp.float32)],
        compiler_params=pltpu.CompilerParams(vmem_limit_bytes=32 * 1024 * 1024),
        name=name,
    )(blocks, start_t)


def body(snapshot, start_one, start_two):
    start_two = start_two.reshape(GY, 16, RANK).transpose(2, 1, 0).reshape(RANK, I2)
    fibers, blocks = exchange(first_kernel, "first", 0, [(I1, COLS), (GROWS, 128)], FIRST)(snapshot)
    basis_one = refine(blocks, start_one.T, 1.0 / (I2 * COLS), "refine_one")
    fibers_two, blocks = exchange(second_kernel, "second", 1, [(I2, 128), (GROWS, 128)], SECOND)(basis_one, fibers)
    basis_two = refine(blocks, start_two, 1.0 / (RANK * COLS), "refine_two")
    core_tensor = exchange(third_kernel, "third", 2, [(6, 3, COLS)], THIRD)(basis_two, fibers_two)
    basis_two = basis_two.reshape(RANK, 16, GY).transpose(2, 1, 0).reshape(I2, RANK)
    return (basis_one.T, basis_two, core_tensor)


def solution(mesh):
    in_specs = (P("gx", "gy", None), P(), P())
    out_specs = (P(), P(), P("gx", "gy", None))
    return jax.shard_map(body, mesh=mesh, in_specs=in_specs, out_specs=out_specs, check_vma=False)
```

```python
import functools

import jax
import jax.numpy as jnp
from jax import lax
from jax.experimental import pallas as pl
from jax.experimental.pallas import tpu as pltpu
from jax.sharding import PartitionSpec as P

I1 = 512
I2 = 512
COLS = 384
RANK = 96
ITERS = 6
GX = 16
GY = 32
NX = 4
NY = 4
BLOCKS = [(p, q) for p in range(4) for q in range(p, 4)]
GROWS = 128 * len(BLOCKS)
HALF = GROWS // 2
PIECE = HALF // 16
QUARTER = PIECE // 4

MESH = pl.DeviceIdType.MESH
precise = lax.Precision.HIGHEST


def place():
    gx = lax.axis_index("gx")
    gy = lax.axis_index("gy")
    x, z_lo = lax.div(gx, 4), lax.rem(gx, 4)
    z_hi = lax.div(gy, 8)
    y = lax.rem(lax.div(gy, 2), 4)
    core = lax.rem(gy, 2)
    return gx, gy, x, y, z_hi, z_lo, core


def remote(src, dst, send, recv, target):
    return pltpu.make_async_remote_copy(
        src_ref=src, dst_ref=dst, send_sem=send, recv_sem=recv, device_id=target, device_id_type=MESH
    )


def gx_peer(d):
    gx, gy = place()[:2]
    return (lax.rem(gx + d, GX), gy)


def gy_peer(d):
    gx, gy = place()[:2]
    return (gx, lax.bitwise_xor(gy, d))


def sibling():
    gx, gy, *_, core = place()
    return (gx, gy + 1 - 2 * core)


def xy_peer(dx, dy):
    gx, gy, x, y, z_hi, z_lo, core = place()
    px, py = lax.rem(x + dx, NX), lax.rem(y + dy, NY)
    return (px * 4 + z_lo, z_hi * 8 + py * 2 + core), px * 4 + py


def z_lo_peer(d):
    gx, gy, x, y, z_hi, z_lo, core = place()
    other = lax.rem(z_lo + d, 4)
    return (x * 4 + other, gy), other


def z_hi_peer(d):
    gx, gy, x, y, z_hi, z_lo, core = place()
    return (gx, lax.rem(z_hi + d, 4) * 8 + y * 2 + core)


def greet(peers):
    barrier = pltpu.get_barrier_semaphore()
    for peer in peers:
        pl.semaphore_signal(barrier, inc=1, device_id=peer, device_id_type=MESH)


def await_greetings(count):
    pl.semaphore_wait(pltpu.get_barrier_semaphore(), count)


XY = [(dx, dy) for dx in range(NX) for dy in range(NY) if (dx, dy) != (0, 0)]


def all_reduce(gp, total, s):
    gx, gy, x, y, z_hi, z_lo, core = place()
    mine = pl.multiple_of(core * HALF, 8)
    other = pl.multiple_of((1 - core) * HALF, 8)
    done = []
    copy = remote(gp.at[pl.ds(other, HALF)], s["rc"], s["c1s"], s["c1r"], sibling())
    copy.start()
    copy.wait_recv()
    done.append(copy)
    s["h"][...] = gp[pl.ds(mine, HALF)] + s["rc"][...]
    copies = []
    for o, (dx, dy) in enumerate(XY):
        peer, q = xy_peer(dx, dy)
        copy = remote(
            s["h"].at[pl.ds(pl.multiple_of(q * PIECE, 8), PIECE)],
            s["rxy"].at[o], s["x1s"].at[o], s["x1r"].at[o], peer,
        )
        copy.start()
        copies.append(copy)
    me = x * 4 + y
    acc = s["h"][pl.ds(pl.multiple_of(me * PIECE, 8), PIECE)]
    for o, copy in enumerate(copies):
        copy.wait_recv()
        acc = acc + s["rxy"][o]
    done += copies
    for i in range(4):
        s["za"][i] = acc[QUARTER * i : QUARTER * (i + 1)]
    copies = []
    for d in range(1, 4):
        peer, other = z_lo_peer(d)
        copy = remote(s["za"].at[other], s["rzl"].at[d - 1], s["z1s"].at[d - 1], s["z1r"].at[d - 1], peer)
        copy.start()
        copies.append(copy)
    part = s["za"][z_lo]
    for d, copy in enumerate(copies):
        copy.wait_recv()
        part = part + s["rzl"][d]
    done += copies
    s["zh"][z_hi] = part
    copies = []
    for d in range(1, 4):
        copy = remote(s["zh"].at[z_hi], s["zh"].at[z_hi], s["z2s"].at[d - 1], s["z2r"].at[d - 1], z_hi_peer(d))
        copy.start()
        copies.append(copy)
    for copy in copies:
        copy.wait_recv()
    done += copies
    s["zl"][z_lo] = (s["zh"][0] + s["zh"][1]) + (s["zh"][2] + s["zh"][3])
    copies = []
    for d in range(1, 4):
        peer, _ = z_lo_peer(d)
        copy = remote(s["zl"].at[z_lo], s["zl"].at[z_lo], s["z3s"].at[d - 1], s["z3r"].at[d - 1], peer)
        copy.start()
        copies.append(copy)
    for copy in copies:
        copy.wait_recv()
    done += copies
    s["agz"][...] = jnp.concatenate([s["zl"][i] for i in range(4)], axis=0)
    own = pl.ds(pl.multiple_of(mine + me * PIECE, 8), PIECE)
    copies = []
    for o, (dx, dy) in enumerate(XY):
        peer, q = xy_peer(dx, dy)
        copy = remote(s["agz"], total.at[own], s["x2s"].at[o], s["x2r"].at[o], peer)
        copy.start()
        copies.append(copy)
    total[own] = s["agz"][...]
    for copy in copies:
        copy.wait_recv()
    done += copies
    copy = remote(total.at[pl.ds(mine, HALF)], total.at[pl.ds(mine, HALF)], s["c2s"], s["c2r"], sibling())
    copy.start()
    copy.wait_recv()
    done.append(copy)
    for copy in done:
        copy.wait_send()


DMA = pltpu.SemaphoreType.DMA
REDUCE = dict(
    gp=pltpu.VMEM((GROWS, 128), jnp.float32),
    total=pltpu.VMEM((GROWS, 128), jnp.float32),
    rc=pltpu.VMEM((HALF, 128), jnp.float32),
    h=pltpu.VMEM((HALF, 128), jnp.float32),
    rxy=pltpu.VMEM((15, PIECE, 128), jnp.float32),
    za=pltpu.VMEM((4, QUARTER, 128), jnp.float32),
    rzl=pltpu.VMEM((3, QUARTER, 128), jnp.float32),
    zh=pltpu.VMEM((4, QUARTER, 128), jnp.float32),
    zl=pltpu.VMEM((4, QUARTER, 128), jnp.float32),
    agz=pltpu.VMEM((PIECE, 128), jnp.float32),
    c1s=DMA, c1r=DMA, c2s=DMA, c2r=DMA,
    x1s=DMA((15,)), x1r=DMA((15,)), x2s=DMA((15,)), x2r=DMA((15,)),
    z1s=DMA((3,)), z1r=DMA((3,)), z2s=DMA((3,)), z2r=DMA((3,)), z3s=DMA((3,)), z3r=DMA((3,)),
)


def gram_blocks(flat, gp):
    n = 0
    for p in range(4):
        strip = lax.dot_general(
            flat[128 * p : 128 * (p + 1)], flat[128 * p :], (((1,), (1,)), ((), ())),
            precision=precise, preferred_element_type=jnp.float32,
        )
        for q in range(4 - p):
            gp[128 * n : 128 * (n + 1)] = strip[:, 128 * q : 128 * (q + 1)]
            n += 1


def swap_granules(tiles):
    lane = lax.broadcasted_iota(jnp.int32, tiles[0].shape, 1)
    tiles = list(tiles)
    for bit in range(4):
        shift = 8 << bit
        low = lax.bitwise_and(lane, shift) == 0
        for j in range(16):
            if not j >> bit & 1:
                k = j | 1 << bit
                a, b = tiles[j], tiles[k]
                tiles[j] = jnp.where(low, a, pltpu.roll(b, shift, 1))
                tiles[k] = jnp.where(low, pltpu.roll(a, 128 - shift, 1), b)
    return tiles


def plane_peers():
    return [xy_peer(dx, dy)[0] for dx in range(1, NX) for dy in range(1, NY)]


def everyone():
    return [gx_peer(d) for d in range(1, GX)] + [gy_peer(d) for d in range(1, GY)] + plane_peers()


def gather_one(x_ref, s):
    gx, gy, *_ = place()
    load = pltpu.make_async_copy(x_ref, s["x"], s["xc"])
    load.start()
    peers = everyone()
    greet(peers)
    load.wait()
    copies = []
    for half in range(2):
        rows = slice(16 * half, 16 * half + 16)
        for c in range(3):
            lanes = slice(128 * c, 128 * (c + 1))
            for g, tile in enumerate(swap_granules([s["x"][rows, j, lanes] for j in range(16)])):
                s["xs"][g, rows, lanes] = tile
        if half == 0:
            await_greetings(len(peers))
        rows = pl.ds(16 * half, 16)
        for d in range(1, GX):
            peer = gx_peer(d)
            copy = remote(
                s["xs"].at[peer[0], rows], s["fib"].at[gx, rows],
                s["as"].at[half, d - 1], s["ar"].at[half, d - 1], peer,
            )
            copy.start()
            copies.append(copy)
    s["fib"][gx] = s["xs"][gx]
    for copy in copies:
        copy.wait_recv()
    return copies


def gather_two(basis_ref, fib_ref, s):
    gx, gy, *_ = place()
    load = pltpu.make_async_copy(fib_ref, s["fib"], s["xc"])
    load.start()
    peers = everyone()
    greet(peers)
    load.wait()
    shrunk = dot(basis_ref[...], s["fib"][...])
    for u in range(GY):
        s["st"][u] = shrunk[3 * u : 3 * (u + 1)]
    await_greetings(len(peers))
    copies = []
    for d in range(1, GY):
        peer = gy_peer(d)
        copy = remote(s["st"].at[peer[1]], s["f2"].at[gy], s["bs"].at[d - 1], s["br"].at[d - 1], peer)
        copy.start()
        copies.append(copy)
    s["f2"][gy] = s["st"][gy]
    for copy in copies:
        copy.wait_recv()
    tiles = [s["f2"][:, a, 128 * c : 128 * (c + 1)] for a in range(3) for c in range(3)]
    tiles += [jnp.zeros((GY, 128), jnp.float32)] * 7
    return jnp.concatenate(swap_granules(tiles), axis=0), copies


def spread_core(basis, columns, out_ref, s):
    gx, gy, *_ = place()
    row, half = lax.div(gy, 2), lax.rem(gy, 2)
    core = dot(basis, columns)
    for u in range(GY):
        s["cs"][u] = core[3 * u : 3 * (u + 1)]
    await_senders()

    def copy(d):
        u = lax.bitwise_xor(gy, d)
        return remote(s["cs"].at[u], s["ro"].at[gx, half], s["ks"].at[d], s["kr"].at[gx, half], (row, u))

    @pl.when(row != gx)
    def _():
        copy(0).start()

    @pl.when(row == gx)
    def _():
        s["ro"][gx, half] = s["cs"][gy]

    for d in range(1, GY):
        copy(d).start()

    def arrival(k, h):
        source = lax.rem(gx + k, GX)
        return remote(s["cs"].at[0], s["ro"].at[source, h], s["ks"].at[0], s["kr"].at[source, h], (source, 2 * gx + h))

    for h in range(2):
        @pl.when(2 * gx + h != gy)
        def _(h=h):
            arrival(0, h).wait_recv()
        for k in range(1, GX):
            arrival(k, h).wait_recv()
    for h in range(2):
        tiles = swap_granules([s["ro"][g, h] for g in range(GX)])
        for a in range(3):
            for c in range(3):
                out_ref[3 * h + a, :, 128 * c : 128 * (c + 1)] = tiles[3 * a + c]

    @pl.when(row != gx)
    def _():
        copy(0).wait_send()

    for d in range(1, GY):
        copy(d).wait_send()


def first_kernel(x_ref, fib_ref, g_ref, s):
    copies = gather_one(x_ref, s)
    flat = s["fib"][...].reshape(I1, COLS)
    fib_ref[...] = flat
    gram_blocks(flat, s["gp"])
    all_reduce(s["gp"], s["total"], s)
    g_ref[...] = s["total"][...]
    for copy in copies:
        copy.wait_send()


def second_kernel(basis_ref, fib_ref, f2_ref, g_ref, s):
    flat, copies = gather_two(basis_ref, fib_ref, s)
    f2_ref[...] = flat
    gram_blocks(flat, s["gp"])
    all_reduce(s["gp"], s["total"], s)
    g_ref[...] = s["total"][...]
    for copy in copies:
        copy.wait_send()


def greet_senders():
    gx, gy, *_ = place()
    barrier = pltpu.get_barrier_semaphore()
    for h in range(2):
        @pl.when(2 * gx + h != gy)
        def _(h=h):
            pl.semaphore_signal(barrier, inc=1, device_id=(gx, 2 * gx + h), device_id_type=MESH)
        for k in range(1, GX):
            pl.semaphore_signal(barrier, inc=1, device_id=(lax.rem(gx + k, GX), 2 * gx + h), device_id_type=MESH)


def await_senders():
    gx, gy, *_ = place()

    @pl.when(lax.div(gy, 2) == gx)
    def _():
        await_greetings(31)

    @pl.when(lax.div(gy, 2) != gx)
    def _():
        await_greetings(32)


def third_kernel(basis_ref, f2_ref, out_ref, s):
    greet_senders()
    spread_core(basis_ref[...], f2_ref[...], out_ref, s)


FIRST = REDUCE | dict(
    x=pltpu.VMEM((32, 16, COLS), jnp.float32), xc=DMA,
    xs=pltpu.VMEM((GX, 32, COLS), jnp.float32), fib=pltpu.VMEM((GX, 32, COLS), jnp.float32),
    **{"as": DMA((2, 15)), "ar": DMA((2, 15))},
)
SECOND = REDUCE | dict(
    fib=pltpu.VMEM((I1, COLS), jnp.float32), xc=DMA,
    st=pltpu.VMEM((GY, 3, COLS), jnp.float32), f2=pltpu.VMEM((GY, 3, COLS), jnp.float32),
    bs=DMA((31,)), br=DMA((31,)),
)
THIRD = dict(
    cs=pltpu.VMEM((GY, 3, 128), jnp.float32), ro=pltpu.VMEM((GX, 2, 3, 128), jnp.float32),
    ks=DMA((32,)), kr=DMA((GX, 2)),
)

VMEM = pl.BlockSpec(memory_space=pltpu.VMEM)
ANY = pl.BlockSpec(memory_space=pl.ANY)


def exchange(kernel, name, ident, ins, outs, scratch):
    def body(*refs):
        count = len(refs) - 1
        kernel(*refs[:count], refs[count])

    def call(*args):
        single = len(outs) == 1
        shapes = [jax.ShapeDtypeStruct(o, jnp.float32) for o in outs]
        return pl.pallas_call(
            body,
            out_shape=shapes[0] if single else shapes,
            in_specs=ins,
            out_specs=VMEM if single else [VMEM] * len(outs),
            scratch_shapes=[scratch],
            compiler_params=pltpu.CompilerParams(
                collective_id=ident, has_side_effects=True, vmem_limit_bytes=32 * 1024 * 1024
            ),
            name=name,
        )(*args)

    return call


def dot(a, b, dims=((1,), (0,))):
    return lax.dot_general(a, b, (dims, ((), ())), precision=precise, preferred_element_type=jnp.float32)


def inverse_factor(c, beside=()):
    lane = lax.broadcasted_iota(jnp.int32, (8, 128), 1)
    row = lax.broadcasted_iota(jnp.int32, (8, 128), 0)
    tiles = [c[8 * i : 8 * (i + 1)] for i in range(RANK // 8)]
    result = []

    def spread_lane(tile, n):
        return jnp.broadcast_to(tile[:, n : n + 1], (8, 128))

    def spread_row(tile, n):
        return jnp.broadcast_to(tile[n : n + 1, :], (8, 128))

    last = RANK // 8 - 1
    own = [spread_lane(tiles[0], t) for t in range(8)]
    for k in range(RANK // 8):
        lo = 8 * k
        near = min(k + 2, last)
        inside = (lane >= lo) & (lane < lo + 8)
        y = [[spread_lane(tiles[i], lo + t) for t in range(8)] for i in range(k + 1, near + 1)]
        if k < last:
            coming = [spread_lane(tiles[k + 1], lo + 8 + t) for t in range(8)]
        d = [[spread_row(own[t], s) for t in range(s + 1)] for s in range(8)]
        unit = jnp.where(inside, jnp.where(lane - lo == row, 1.0, 0.0), tiles[k])
        p = [spread_row(unit, s) for s in range(8)]
        if k in (2, 6) and beside:
            beside[(2, 6).index(k)]()
        rd = [None] * 8
        m = [[None] * 8 for _ in range(8)]
        for t in range(8):
            rd[t] = 1.0 / d[t][t]
            for s in range(t + 1, 8):
                m[s][t] = d[s][t] * rd[t]
                for u in range(t + 1, s + 1):
                    d[s][u] = d[s][u] - m[s][t] * d[u][t]
                p[s] = p[s] - m[s][t] * p[t]
                for col in y:
                    col[s] = col[s] - m[s][t] * col[t]
        rows = p[0] * lax.rsqrt(d[0][0])
        for s in range(1, 8):
            rows = jnp.where(row == s, p[s] * lax.rsqrt(d[s][s]), rows)
        result.append(jnp.where(lane < lo + 8, rows, 0.0))
        if k == last:
            break
        scaled = [[col[t] * rd[t] for t in range(8)] for col in y]
        own = list(coming)
        for u in range(8):
            for t in range(8):
                own[u] = own[u] - scaled[0][t] * spread_row(y[0][t], u)
        if near < last:
            q = [p[t] * rd[t] for t in range(8)]
            for s in range(7, 0, -1):
                for t in range(s):
                    q[t] = q[t] - m[s][t] * q[s]
            picked = q[0]
            for t in range(1, 8):
                picked = jnp.where(row == t, q[t], picked)
            spread = [picked] if k == 0 else [jnp.zeros((lo, 128), jnp.float32), picked]
            spread = jnp.concatenate(spread + [jnp.zeros((120 - lo, 128), jnp.float32)], axis=0)
            change = dot(jnp.concatenate(tiles[near + 1 :], axis=0), spread)
        for i in range(k + 1, last + 1):
            new = jnp.where(inside, 0.0, tiles[i])
            if i <= near:
                for t in range(8):
                    new = new - scaled[i - k - 1][t] * p[t]
            else:
                at = 8 * (i - near - 1)
                new = new - change[at : at + 8]
            tiles[i] = new
    return jnp.concatenate(result, axis=0)


def refine_kernel(scale, blocks_ref, start_ref, out_ref, g_ref):
    for n, (p, q) in enumerate(BLOCKS):
        block = blocks_ref[128 * n : 128 * (n + 1)] * scale
        g_ref[128 * p : 128 * (p + 1), 128 * q : 128 * (q + 1)] = block
        if p != q:
            g_ref[128 * q : 128 * (q + 1), 128 * p : 128 * (p + 1)] = block.T
    pad = jnp.zeros((128 - RANK, 512), jnp.float32)

    def factor(images, beside=()):
        full = jnp.concatenate([images, pad], axis=0)
        return inverse_factor(dot(images, full, ((1,), (1,))), beside)

    def sweep(_, images):
        ahead = []

        def column(n):
            return lambda: ahead.append(dot(images, g_ref[:, 256 * n : 256 * (n + 1)]))

        inverse = factor(images, [column(n) for n in range(2)])
        return dot(inverse, jnp.concatenate([jnp.concatenate(ahead, axis=1), pad], axis=0))

    images = dot(start_ref[...], g_ref[...])
    images = lax.fori_loop(0, ITERS - 1, sweep, images)
    out_ref[...] = dot(factor(images), jnp.concatenate([images, pad], axis=0))


def refine(blocks, start_t, scale, name):
    vmem = pl.BlockSpec(memory_space=pltpu.VMEM)
    return pl.pallas_call(
        functools.partial(refine_kernel, scale),
        out_shape=jax.ShapeDtypeStruct((RANK, 512), jnp.float32),
        in_specs=[vmem] * 2,
        out_specs=vmem,
        scratch_shapes=[pltpu.VMEM((512, 512), jnp.float32)],
        compiler_params=pltpu.CompilerParams(vmem_limit_bytes=32 * 1024 * 1024),
        name=name,
    )(blocks, start_t)


def body(snapshot, start_one, start_two):
    start_two = start_two.reshape(GY, 16, RANK).transpose(2, 1, 0).reshape(RANK, I2)
    fibers, blocks = exchange(first_kernel, "first", 0, [ANY], [(I1, COLS), (GROWS, 128)], FIRST)(snapshot)
    basis_one = refine(blocks, start_one.T, 1.0 / (I2 * COLS), "refine_one")
    fibers_two, blocks = exchange(second_kernel, "second", 1, [VMEM, ANY], [(I2, 128), (GROWS, 128)], SECOND)(basis_one, fibers)
    basis_two = refine(blocks, start_two, 1.0 / (RANK * COLS), "refine_two")
    core_tensor = exchange(third_kernel, "third", 2, [VMEM, VMEM], [(6, 3, COLS)], THIRD)(basis_two, fibers_two)
    basis_two = basis_two.reshape(RANK, 16, GY).transpose(2, 1, 0).reshape(I2, RANK)
    return (basis_one.T, basis_two, core_tensor)


def solution(mesh):
    in_specs = (P("gx", "gy", None), P(), P())
    out_specs = (P(), P(), P("gx", "gy", None))
    return jax.shard_map(body, mesh=mesh, in_specs=in_specs, out_specs=out_specs, check_vma=False)
```

```python
import functools

import jax
import jax.numpy as jnp
from jax import lax
from jax.experimental import pallas as pl
from jax.experimental.pallas import tpu as pltpu
from jax.sharding import PartitionSpec as P

I1 = 512
I2 = 512
COLS = 384
RANK = 96
ITERS = 6
GX = 16
GY = 32
NX = 4
NY = 4
BLOCKS = [(p, q) for p in range(4) for q in range(p, 4)]
GROWS = 128 * len(BLOCKS)
HALF = GROWS // 2
PIECE = HALF // 16
QUARTER = PIECE // 4

MESH = pl.DeviceIdType.MESH
precise = lax.Precision.HIGHEST


def place():
    gx = lax.axis_index("gx")
    gy = lax.axis_index("gy")
    x, z_lo = lax.div(gx, 4), lax.rem(gx, 4)
    z_hi = lax.div(gy, 8)
    y = lax.rem(lax.div(gy, 2), 4)
    core = lax.rem(gy, 2)
    return gx, gy, x, y, z_hi, z_lo, core


def remote(src, dst, send, recv, target):
    return pltpu.make_async_remote_copy(
        src_ref=src, dst_ref=dst, send_sem=send, recv_sem=recv, device_id=target, device_id_type=MESH
    )


def gx_peer(d):
    gx, gy = place()[:2]
    return (lax.rem(gx + d, GX), gy)


def gy_peer(d):
    gx, gy = place()[:2]
    return (gx, lax.bitwise_xor(gy, d))


def sibling():
    gx, gy, *_, core = place()
    return (gx, gy + 1 - 2 * core)


def xy_peer(dx, dy):
    gx, gy, x, y, z_hi, z_lo, core = place()
    px, py = lax.rem(x + dx, NX), lax.rem(y + dy, NY)
    return (px * 4 + z_lo, z_hi * 8 + py * 2 + core), px * 4 + py


def z_lo_peer(d):
    gx, gy, x, y, z_hi, z_lo, core = place()
    other = lax.rem(z_lo + d, 4)
    return (x * 4 + other, gy), other


def z_hi_peer(d):
    gx, gy, x, y, z_hi, z_lo, core = place()
    return (gx, lax.rem(z_hi + d, 4) * 8 + y * 2 + core)


def greet(peers):
    barrier = pltpu.get_barrier_semaphore()
    for peer in peers:
        pl.semaphore_signal(barrier, inc=1, device_id=peer, device_id_type=MESH)


def await_greetings(count):
    pl.semaphore_wait(pltpu.get_barrier_semaphore(), count)


XY = [(dx, dy) for dx in range(NX) for dy in range(NY) if (dx, dy) != (0, 0)]


def all_reduce(gp, total, s):
    gx, gy, x, y, z_hi, z_lo, core = place()
    mine = pl.multiple_of(core * HALF, 8)
    other = pl.multiple_of((1 - core) * HALF, 8)
    done = []
    copy = remote(gp.at[pl.ds(other, HALF)], s["rc"], s["c1s"], s["c1r"], sibling())
    copy.start()
    copy.wait_recv()
    done.append(copy)
    s["h"][...] = gp[pl.ds(mine, HALF)] + s["rc"][...]
    copies = []
    for o, (dx, dy) in enumerate(XY):
        peer, q = xy_peer(dx, dy)
        copy = remote(
            s["h"].at[pl.ds(pl.multiple_of(q * PIECE, 8), PIECE)],
            s["rxy"].at[o], s["x1s"].at[o], s["x1r"].at[o], peer,
        )
        copy.start()
        copies.append(copy)
    me = x * 4 + y
    acc = s["h"][pl.ds(pl.multiple_of(me * PIECE, 8), PIECE)]
    for o, copy in enumerate(copies):
        copy.wait_recv()
        acc = acc + s["rxy"][o]
    done += copies
    for i in range(4):
        s["za"][i] = acc[QUARTER * i : QUARTER * (i + 1)]
    copies = []
    for d in range(1, 4):
        peer, other = z_lo_peer(d)
        copy = remote(s["za"].at[other], s["rzl"].at[d - 1], s["z1s"].at[d - 1], s["z1r"].at[d - 1], peer)
        copy.start()
        copies.append(copy)
    part = s["za"][z_lo]
    for d, copy in enumerate(copies):
        copy.wait_recv()
        part = part + s["rzl"][d]
    done += copies
    s["zh"][z_hi] = part
    copies = []
    for d in range(1, 4):
        copy = remote(s["zh"].at[z_hi], s["zh"].at[z_hi], s["z2s"].at[d - 1], s["z2r"].at[d - 1], z_hi_peer(d))
        copy.start()
        copies.append(copy)
    for copy in copies:
        copy.wait_recv()
    done += copies
    s["zl"][z_lo] = (s["zh"][0] + s["zh"][1]) + (s["zh"][2] + s["zh"][3])
    copies = []
    for d in range(1, 4):
        peer, _ = z_lo_peer(d)
        copy = remote(s["zl"].at[z_lo], s["zl"].at[z_lo], s["z3s"].at[d - 1], s["z3r"].at[d - 1], peer)
        copy.start()
        copies.append(copy)
    for copy in copies:
        copy.wait_recv()
    done += copies
    s["agz"][...] = jnp.concatenate([s["zl"][i] for i in range(4)], axis=0)
    own = pl.ds(pl.multiple_of(mine + me * PIECE, 8), PIECE)
    copies = []
    for o, (dx, dy) in enumerate(XY):
        peer, q = xy_peer(dx, dy)
        copy = remote(s["agz"], total.at[own], s["x2s"].at[o], s["x2r"].at[o], peer)
        copy.start()
        copies.append(copy)
    total[own] = s["agz"][...]
    for copy in copies:
        copy.wait_recv()
    done += copies
    copy = remote(total.at[pl.ds(mine, HALF)], total.at[pl.ds(mine, HALF)], s["c2s"], s["c2r"], sibling())
    copy.start()
    copy.wait_recv()
    done.append(copy)
    for copy in done:
        copy.wait_send()


DMA = pltpu.SemaphoreType.DMA
REDUCE = dict(
    gp=pltpu.VMEM((GROWS, 128), jnp.float32),
    total=pltpu.VMEM((GROWS, 128), jnp.float32),
    rc=pltpu.VMEM((HALF, 128), jnp.float32),
    h=pltpu.VMEM((HALF, 128), jnp.float32),
    rxy=pltpu.VMEM((15, PIECE, 128), jnp.float32),
    za=pltpu.VMEM((4, QUARTER, 128), jnp.float32),
    rzl=pltpu.VMEM((3, QUARTER, 128), jnp.float32),
    zh=pltpu.VMEM((4, QUARTER, 128), jnp.float32),
    zl=pltpu.VMEM((4, QUARTER, 128), jnp.float32),
    agz=pltpu.VMEM((PIECE, 128), jnp.float32),
    c1s=DMA, c1r=DMA, c2s=DMA, c2r=DMA,
    x1s=DMA((15,)), x1r=DMA((15,)), x2s=DMA((15,)), x2r=DMA((15,)),
    z1s=DMA((3,)), z1r=DMA((3,)), z2s=DMA((3,)), z2r=DMA((3,)), z3s=DMA((3,)), z3r=DMA((3,)),
)


def gram_blocks(flat, gp):
    n = 0
    for p in range(4):
        strip = lax.dot_general(
            flat[128 * p : 128 * (p + 1)], flat[128 * p :], (((1,), (1,)), ((), ())),
            precision=precise, preferred_element_type=jnp.float32,
        )
        for q in range(4 - p):
            gp[128 * n : 128 * (n + 1)] = strip[:, 128 * q : 128 * (q + 1)]
            n += 1


def swap_granules(tiles):
    lane = lax.broadcasted_iota(jnp.int32, tiles[0].shape, 1)
    tiles = list(tiles)
    for bit in range(4):
        shift = 8 << bit
        low = lax.bitwise_and(lane, shift) == 0
        for j in range(16):
            if not j >> bit & 1:
                k = j | 1 << bit
                a, b = tiles[j], tiles[k]
                tiles[j] = jnp.where(low, a, pltpu.roll(b, shift, 1))
                tiles[k] = jnp.where(low, pltpu.roll(a, 128 - shift, 1), b)
    return tiles


def plane_peers():
    return [xy_peer(dx, dy)[0] for dx in range(1, NX) for dy in range(1, NY)]


def everyone():
    return [gx_peer(d) for d in range(1, GX)] + [gy_peer(d) for d in range(1, GY)] + plane_peers()


def gather_one(x_ref, s):
    gx, gy, *_ = place()
    load = pltpu.make_async_copy(x_ref, s["x"], s["xc"])
    load.start()
    peers = everyone()
    greet(peers)
    load.wait()
    copies = []
    for half in range(2):
        rows = slice(16 * half, 16 * half + 16)
        for c in range(3):
            lanes = slice(128 * c, 128 * (c + 1))
            for g, tile in enumerate(swap_granules([s["x"][rows, j, lanes] for j in range(16)])):
                s["xs"][g, rows, lanes] = tile
        if half == 0:
            await_greetings(len(peers))
        rows = pl.ds(16 * half, 16)
        for d in range(1, GX):
            peer = gx_peer(d)
            copy = remote(
                s["xs"].at[peer[0], rows], s["fib"].at[gx, rows],
                s["as"].at[half, d - 1], s["ar"].at[half, d - 1], peer,
            )
            copy.start()
            copies.append(copy)
    s["fib"][gx] = s["xs"][gx]
    for copy in copies:
        copy.wait_recv()
    return copies


def gather_two(blocks_ref, start_ref, basis_ref, fib_ref, s):
    gx, gy, *_ = place()
    load = pltpu.make_async_copy(fib_ref, s["fib"], s["xc"])
    load.start()
    peers = everyone()
    greet(peers)
    refine_into(1.0 / (I2 * COLS), blocks_ref, start_ref, basis_ref, s["g"], s["last"], s["inverse"])
    load.wait()
    shrunk = dot(basis_ref[...], s["fib"][...])
    for u in range(GY):
        s["st"][u] = shrunk[3 * u : 3 * (u + 1)]
    await_greetings(len(peers))
    copies = []
    for d in range(1, GY):
        peer = gy_peer(d)
        copy = remote(s["st"].at[peer[1]], s["f2"].at[gy], s["bs"].at[d - 1], s["br"].at[d - 1], peer)
        copy.start()
        copies.append(copy)
    s["f2"][gy] = s["st"][gy]
    for copy in copies:
        copy.wait_recv()
    tiles = [s["f2"][:, a, 128 * c : 128 * (c + 1)] for a in range(3) for c in range(3)]
    tiles += [jnp.zeros((GY, 128), jnp.float32)] * 7
    return jnp.concatenate(swap_granules(tiles), axis=0), copies


def spread_core(basis, columns, out_ref, s):
    gx, gy, *_ = place()
    row, half = lax.div(gy, 2), lax.rem(gy, 2)
    core = dot(basis, columns)
    for u in range(GY):
        s["cs"][u] = core[3 * u : 3 * (u + 1)]
    await_senders()

    def copy(d):
        u = lax.bitwise_xor(gy, d)
        return remote(s["cs"].at[u], s["ro"].at[gx, half], s["ks"].at[d], s["kr"].at[gx, half], (row, u))

    @pl.when(row != gx)
    def _():
        copy(0).start()

    @pl.when(row == gx)
    def _():
        s["ro"][gx, half] = s["cs"][gy]

    for d in range(1, GY):
        copy(d).start()

    def arrival(k, h):
        source = lax.rem(gx + k, GX)
        return remote(s["cs"].at[0], s["ro"].at[source, h], s["ks"].at[0], s["kr"].at[source, h], (source, 2 * gx + h))

    for h in range(2):
        @pl.when(2 * gx + h != gy)
        def _(h=h):
            arrival(0, h).wait_recv()
        for k in range(1, GX):
            arrival(k, h).wait_recv()
    for h in range(2):
        tiles = swap_granules([s["ro"][g, h] for g in range(GX)])
        for a in range(3):
            for c in range(3):
                out_ref[3 * h + a, :, 128 * c : 128 * (c + 1)] = tiles[3 * a + c]

    @pl.when(row != gx)
    def _():
        copy(0).wait_send()

    for d in range(1, GY):
        copy(d).wait_send()


def first_kernel(x_ref, fib_ref, g_ref, s):
    copies = gather_one(x_ref, s)
    flat = s["fib"][...].reshape(I1, COLS)
    fib_ref[...] = flat
    gram_blocks(flat, s["gp"])
    all_reduce(s["gp"], s["total"], s)
    g_ref[...] = s["total"][...]
    for copy in copies:
        copy.wait_send()


def second_kernel(blocks_ref, start_ref, fib_ref, basis_ref, f2_ref, g_ref, s):
    flat, copies = gather_two(blocks_ref, start_ref, basis_ref, fib_ref, s)
    f2_ref[...] = flat
    gram_blocks(flat, s["gp"])
    all_reduce(s["gp"], s["total"], s)
    g_ref[...] = s["total"][...]
    for copy in copies:
        copy.wait_send()


def greet_senders():
    gx, gy, *_ = place()
    barrier = pltpu.get_barrier_semaphore()
    for h in range(2):
        @pl.when(2 * gx + h != gy)
        def _(h=h):
            pl.semaphore_signal(barrier, inc=1, device_id=(gx, 2 * gx + h), device_id_type=MESH)
        for k in range(1, GX):
            pl.semaphore_signal(barrier, inc=1, device_id=(lax.rem(gx + k, GX), 2 * gx + h), device_id_type=MESH)


def await_senders():
    gx, gy, *_ = place()

    @pl.when(lax.div(gy, 2) == gx)
    def _():
        await_greetings(31)

    @pl.when(lax.div(gy, 2) != gx)
    def _():
        await_greetings(32)


def third_kernel(blocks_ref, start_ref, f2_ref, basis_ref, out_ref, s):
    greet_senders()
    refine_into(1.0 / (RANK * COLS), blocks_ref, start_ref, basis_ref, s["g"], s["last"], s["inverse"])
    spread_core(basis_ref[...], f2_ref[...], out_ref, s)


FIRST = REDUCE | dict(
    x=pltpu.VMEM((32, 16, COLS), jnp.float32), xc=DMA,
    xs=pltpu.VMEM((GX, 32, COLS), jnp.float32), fib=pltpu.VMEM((GX, 32, COLS), jnp.float32),
    **{"as": DMA((2, 15)), "ar": DMA((2, 15))},
)
SECOND = REDUCE | dict(
    g=pltpu.VMEM((I1, I1), jnp.float32), last=pltpu.VMEM((RANK, I1), jnp.float32),
    inverse=pltpu.VMEM((RANK, 128), jnp.float32),
    fib=pltpu.VMEM((I1, COLS), jnp.float32), xc=DMA,
    st=pltpu.VMEM((GY, 3, COLS), jnp.float32), f2=pltpu.VMEM((GY, 3, COLS), jnp.float32),
    bs=DMA((31,)), br=DMA((31,)),
)
THIRD = dict(
    g=pltpu.VMEM((I1, I1), jnp.float32), last=pltpu.VMEM((RANK, I1), jnp.float32),
    inverse=pltpu.VMEM((RANK, 128), jnp.float32),
    cs=pltpu.VMEM((GY, 3, 128), jnp.float32), ro=pltpu.VMEM((GX, 2, 3, 128), jnp.float32),
    ks=DMA((32,)), kr=DMA((GX, 2)),
)

VMEM = pl.BlockSpec(memory_space=pltpu.VMEM)
ANY = pl.BlockSpec(memory_space=pltpu.HBM)


def exchange(kernel, name, ident, ins, outs, scratch):
    def body(*refs):
        count = len(refs) - 1
        kernel(*refs[:count], refs[count])

    def call(*args):
        single = len(outs) == 1
        shapes = [jax.ShapeDtypeStruct(o, jnp.float32) for o in outs]
        return pl.pallas_call(
            body,
            out_shape=shapes[0] if single else shapes,
            in_specs=ins,
            out_specs=VMEM if single else [VMEM] * len(outs),
            scratch_shapes=[scratch],
            compiler_params=pltpu.CompilerParams(
                collective_id=ident, has_side_effects=True, vmem_limit_bytes=32 * 1024 * 1024
            ),
            name=name,
        )(*args)

    return call


def dot(a, b, dims=((1,), (0,))):
    return lax.dot_general(a, b, (dims, ((), ())), precision=precise, preferred_element_type=jnp.float32)


def inverse_factor(c, beside=()):
    lane = lax.broadcasted_iota(jnp.int32, (8, 128), 1)
    row = lax.broadcasted_iota(jnp.int32, (8, 128), 0)
    tiles = [c[8 * i : 8 * (i + 1)] for i in range(RANK // 8)]
    result = []

    def spread_lane(tile, n):
        return jnp.broadcast_to(tile[:, n : n + 1], (8, 128))

    def spread_row(tile, n):
        return jnp.broadcast_to(tile[n : n + 1, :], (8, 128))

    last = RANK // 8 - 1
    own = [spread_lane(tiles[0], t) for t in range(8)]
    for k in range(RANK // 8):
        lo = 8 * k
        near = min(k + 2, last)
        inside = (lane >= lo) & (lane < lo + 8)
        y = [[spread_lane(tiles[i], lo + t) for t in range(8)] for i in range(k + 1, near + 1)]
        if k < last:
            coming = [spread_lane(tiles[k + 1], lo + 8 + t) for t in range(8)]
        d = [[spread_row(own[t], s) for t in range(s + 1)] for s in range(8)]
        unit = jnp.where(inside, jnp.where(lane - lo == row, 1.0, 0.0), tiles[k])
        p = [spread_row(unit, s) for s in range(8)]
        if k in (2, 6) and beside:
            beside[(2, 6).index(k)]()
        rd = [None] * 8
        m = [[None] * 8 for _ in range(8)]
        for t in range(8):
            rd[t] = 1.0 / d[t][t]
            for s in range(t + 1, 8):
                m[s][t] = d[s][t] * rd[t]
                for u in range(t + 1, s + 1):
                    d[s][u] = d[s][u] - m[s][t] * d[u][t]
                p[s] = p[s] - m[s][t] * p[t]
                for col in y:
                    col[s] = col[s] - m[s][t] * col[t]
        rows = p[0] * lax.rsqrt(d[0][0])
        for s in range(1, 8):
            rows = jnp.where(row == s, p[s] * lax.rsqrt(d[s][s]), rows)
        result.append(jnp.where(lane < lo + 8, rows, 0.0))
        if k == last:
            break
        scaled = [[col[t] * rd[t] for t in range(8)] for col in y]
        own = list(coming)
        for u in range(8):
            for t in range(8):
                own[u] = own[u] - scaled[0][t] * spread_row(y[0][t], u)
        if near < last:
            q = [p[t] * rd[t] for t in range(8)]
            for s in range(7, 0, -1):
                for t in range(s):
                    q[t] = q[t] - m[s][t] * q[s]
            picked = q[0]
            for t in range(1, 8):
                picked = jnp.where(row == t, q[t], picked)
            spread = [picked] if k == 0 else [jnp.zeros((lo, 128), jnp.float32), picked]
            spread = jnp.concatenate(spread + [jnp.zeros((120 - lo, 128), jnp.float32)], axis=0)
            change = dot(jnp.concatenate(tiles[near + 1 :], axis=0), spread)
        for i in range(k + 1, last + 1):
            new = jnp.where(inside, 0.0, tiles[i])
            if i <= near:
                for t in range(8):
                    new = new - scaled[i - k - 1][t] * p[t]
            else:
                at = 8 * (i - near - 1)
                new = new - change[at : at + 8]
            tiles[i] = new
    return jnp.concatenate(result, axis=0)


def refine_into(scale, blocks_ref, start_ref, out_ref, g_ref, last_ref, inverse_ref):
    for n, (p, q) in enumerate(BLOCKS):
        block = blocks_ref[128 * n : 128 * (n + 1)] * scale
        g_ref[128 * p : 128 * (p + 1), 128 * q : 128 * (q + 1)] = block
        if p != q:
            g_ref[128 * q : 128 * (q + 1), 128 * p : 128 * (p + 1)] = block.T
    pad = jnp.zeros((128 - RANK, 512), jnp.float32)

    def factor(images, beside=()):
        full = jnp.concatenate([images, pad], axis=0)
        return inverse_factor(dot(images, full, ((1,), (1,))), beside)

    def sweep(_, images):
        ahead = []

        def column(n):
            return lambda: ahead.append(dot(images, g_ref[:, 256 * n : 256 * (n + 1)]))

        inverse = factor(images, [column(n) for n in range(2)])
        last_ref[...] = images
        inverse_ref[...] = inverse
        return dot(inverse, jnp.concatenate([jnp.concatenate(ahead, axis=1), pad], axis=0))

    lax.fori_loop(0, ITERS, sweep, dot(start_ref[...], g_ref[...]))
    out_ref[...] = dot(inverse_ref[...], jnp.concatenate([last_ref[...], pad], axis=0))


def body(snapshot, start_one, start_two):
    start_two = start_two.reshape(GY, 16, RANK).transpose(2, 1, 0).reshape(RANK, I2)
    fibers, blocks = exchange(first_kernel, "first", 0, [ANY], [(I1, COLS), (GROWS, 128)], FIRST)(snapshot)
    basis_one, fibers_two, blocks = exchange(
        second_kernel, "second", 1, [VMEM, VMEM, ANY], [(RANK, I1), (I2, 128), (GROWS, 128)], SECOND
    )(blocks, start_one.T, fibers)
    basis_two, core_tensor = exchange(
        third_kernel, "third", 2, [VMEM] * 3, [(RANK, I2), (6, 3, COLS)], THIRD
    )(blocks, start_two, fibers_two)
    basis_two = basis_two.reshape(RANK, 16, GY).transpose(2, 1, 0).reshape(I2, RANK)
    return (basis_one.T, basis_two, core_tensor)


def solution(mesh):
    in_specs = (P("gx", "gy", None), P(), P())
    out_specs = (P(), P(), P("gx", "gy", None))
    return jax.shard_map(body, mesh=mesh, in_specs=in_specs, out_specs=out_specs, check_vma=False)
```

```python
import functools

import jax
import jax.numpy as jnp
from jax import lax
from jax.experimental import pallas as pl
from jax.experimental.pallas import tpu as pltpu
from jax.sharding import PartitionSpec as P

I1 = 512
I2 = 512
COLS = 384
RANK = 96
ITERS = 6
GX = 16
GY = 32
NX = 4
NY = 4
BLOCKS = [(p, q) for p in range(4) for q in range(p, 4)]
GROWS = 128 * len(BLOCKS)
HALF = GROWS // 2
PIECE = HALF // 16
QUARTER = PIECE // 4

MESH = pl.DeviceIdType.MESH
precise = lax.Precision.HIGHEST


def place():
    gx = lax.axis_index("gx")
    gy = lax.axis_index("gy")
    x, z_lo = lax.div(gx, 4), lax.rem(gx, 4)
    z_hi = lax.div(gy, 8)
    y = lax.rem(lax.div(gy, 2), 4)
    core = lax.rem(gy, 2)
    return gx, gy, x, y, z_hi, z_lo, core


def remote(src, dst, send, recv, target):
    return pltpu.make_async_remote_copy(
        src_ref=src, dst_ref=dst, send_sem=send, recv_sem=recv, device_id=target, device_id_type=MESH
    )


def gx_peer(d):
    gx, gy = place()[:2]
    return (lax.rem(gx + d, GX), gy)


def gy_peer(d):
    gx, gy = place()[:2]
    return (gx, lax.bitwise_xor(gy, d))


def sibling():
    gx, gy, *_, core = place()
    return (gx, gy + 1 - 2 * core)


def xy_peer(dx, dy):
    gx, gy, x, y, z_hi, z_lo, core = place()
    px, py = lax.rem(x + dx, NX), lax.rem(y + dy, NY)
    return (px * 4 + z_lo, z_hi * 8 + py * 2 + core), px * 4 + py


def z_lo_peer(d):
    gx, gy, x, y, z_hi, z_lo, core = place()
    other = lax.rem(z_lo + d, 4)
    return (x * 4 + other, gy), other


def z_hi_peer(d):
    gx, gy, x, y, z_hi, z_lo, core = place()
    return (gx, lax.rem(z_hi + d, 4) * 8 + y * 2 + core)


def greet(peers):
    barrier = pltpu.get_barrier_semaphore()
    for peer in peers:
        pl.semaphore_signal(barrier, inc=1, device_id=peer, device_id_type=MESH)


def await_greetings(count):
    pl.semaphore_wait(pltpu.get_barrier_semaphore(), count)


XY = [(dx, dy) for dx in range(NX) for dy in range(NY) if (dx, dy) != (0, 0)]


def all_reduce(gp, total, s):
    gx, gy, x, y, z_hi, z_lo, core = place()
    mine = pl.multiple_of(core * HALF, 8)
    other = pl.multiple_of((1 - core) * HALF, 8)
    done = []
    copy = remote(gp.at[pl.ds(other, HALF)], s["rc"], s["c1s"], s["c1r"], sibling())
    copy.start()
    copy.wait_recv()
    done.append(copy)
    s["h"][...] = gp[pl.ds(mine, HALF)] + s["rc"][...]
    copies = []
    for o, (dx, dy) in enumerate(XY):
        peer, q = xy_peer(dx, dy)
        copy = remote(
            s["h"].at[pl.ds(pl.multiple_of(q * PIECE, 8), PIECE)],
            s["rxy"].at[o], s["x1s"].at[o], s["x1r"].at[o], peer,
        )
        copy.start()
        copies.append(copy)
    me = x * 4 + y
    acc = s["h"][pl.ds(pl.multiple_of(me * PIECE, 8), PIECE)]
    for o, copy in enumerate(copies):
        copy.wait_recv()
        acc = acc + s["rxy"][o]
    done += copies
    for i in range(4):
        s["za"][i] = acc[QUARTER * i : QUARTER * (i + 1)]
    copies = []
    for d in range(1, 4):
        peer, other = z_lo_peer(d)
        copy = remote(s["za"].at[other], s["rzl"].at[d - 1], s["z1s"].at[d - 1], s["z1r"].at[d - 1], peer)
        copy.start()
        copies.append(copy)
    part = s["za"][z_lo]
    for d, copy in enumerate(copies):
        copy.wait_recv()
        part = part + s["rzl"][d]
    done += copies
    s["zh"][z_hi] = part
    copies = []
    for d in range(1, 4):
        copy = remote(s["zh"].at[z_hi], s["zh"].at[z_hi], s["z2s"].at[d - 1], s["z2r"].at[d - 1], z_hi_peer(d))
        copy.start()
        copies.append(copy)
    for copy in copies:
        copy.wait_recv()
    done += copies
    s["zl"][z_lo] = (s["zh"][0] + s["zh"][1]) + (s["zh"][2] + s["zh"][3])
    copies = []
    for d in range(1, 4):
        peer, _ = z_lo_peer(d)
        copy = remote(s["zl"].at[z_lo], s["zl"].at[z_lo], s["z3s"].at[d - 1], s["z3r"].at[d - 1], peer)
        copy.start()
        copies.append(copy)
    for copy in copies:
        copy.wait_recv()
    done += copies
    s["agz"][...] = jnp.concatenate([s["zl"][i] for i in range(4)], axis=0)
    own = pl.ds(pl.multiple_of(mine + me * PIECE, 8), PIECE)
    copies = []
    for o, (dx, dy) in enumerate(XY):
        peer, q = xy_peer(dx, dy)
        copy = remote(s["agz"], total.at[own], s["x2s"].at[o], s["x2r"].at[o], peer)
        copy.start()
        copies.append(copy)
    total[own] = s["agz"][...]
    for copy in copies:
        copy.wait_recv()
    done += copies
    copy = remote(total.at[pl.ds(mine, HALF)], total.at[pl.ds(mine, HALF)], s["c2s"], s["c2r"], sibling())
    copy.start()
    copy.wait_recv()
    done.append(copy)
    for copy in done:
        copy.wait_send()


DMA = pltpu.SemaphoreType.DMA
REDUCE = dict(
    gp=pltpu.VMEM((GROWS, 128), jnp.float32),
    total=pltpu.VMEM((GROWS, 128), jnp.float32),
    rc=pltpu.VMEM((HALF, 128), jnp.float32),
    h=pltpu.VMEM((HALF, 128), jnp.float32),
    rxy=pltpu.VMEM((15, PIECE, 128), jnp.float32),
    za=pltpu.VMEM((4, QUARTER, 128), jnp.float32),
    rzl=pltpu.VMEM((3, QUARTER, 128), jnp.float32),
    zh=pltpu.VMEM((4, QUARTER, 128), jnp.float32),
    zl=pltpu.VMEM((4, QUARTER, 128), jnp.float32),
    agz=pltpu.VMEM((PIECE, 128), jnp.float32),
    c1s=DMA, c1r=DMA, c2s=DMA, c2r=DMA,
    x1s=DMA((15,)), x1r=DMA((15,)), x2s=DMA((15,)), x2r=DMA((15,)),
    z1s=DMA((3,)), z1r=DMA((3,)), z2s=DMA((3,)), z2r=DMA((3,)), z3s=DMA((3,)), z3r=DMA((3,)),
)


def gram_blocks(flat, gp):
    n = 0
    for p in range(4):
        strip = lax.dot_general(
            flat[128 * p : 128 * (p + 1)], flat[128 * p :], (((1,), (1,)), ((), ())),
            precision=precise, preferred_element_type=jnp.float32,
        )
        for q in range(4 - p):
            gp[128 * n : 128 * (n + 1)] = strip[:, 128 * q : 128 * (q + 1)]
            n += 1


def swap_granules(tiles):
    lane = lax.broadcasted_iota(jnp.int32, tiles[0].shape, 1)
    tiles = list(tiles)
    for bit in range(4):
        shift = 8 << bit
        low = lax.bitwise_and(lane, shift) == 0
        for j in range(16):
            if not j >> bit & 1:
                k = j | 1 << bit
                a, b = tiles[j], tiles[k]
                tiles[j] = jnp.where(low, a, pltpu.roll(b, shift, 1))
                tiles[k] = jnp.where(low, pltpu.roll(a, 128 - shift, 1), b)
    return tiles


def plane_peers():
    return [xy_peer(dx, dy)[0] for dx in range(1, NX) for dy in range(1, NY)]


def everyone():
    return [gx_peer(d) for d in range(1, GX)] + [gy_peer(d) for d in range(1, GY)] + plane_peers()


def gather_one(x_ref, s):
    gx, gy, *_ = place()
    load = pltpu.make_async_copy(x_ref, s["x"], s["xc"])
    load.start()
    peers = everyone()
    greet(peers)
    greet_senders()
    load.wait()
    copies = []
    for half in range(2):
        rows = slice(16 * half, 16 * half + 16)
        for c in range(3):
            lanes = slice(128 * c, 128 * (c + 1))
            for g, tile in enumerate(swap_granules([s["x"][rows, j, lanes] for j in range(16)])):
                s["xs"][g, rows, lanes] = tile
        if half == 0:
            await_everyone(len(peers))
        rows = pl.ds(16 * half, 16)
        for d in range(1, GX):
            peer = gx_peer(d)
            copy = remote(
                s["xs"].at[peer[0], rows], s["fib"].at[gx, rows],
                s["as"].at[half, d - 1], s["ar"].at[half, d - 1], peer,
            )
            copy.start()
            copies.append(copy)
    s["fib"][gx] = s["xs"][gx]
    for copy in copies:
        copy.wait_recv()
    return copies


def gather_two(basis_ref, fibers, s):
    gx, gy, *_ = place()
    shrunk = dot(basis_ref[...], fibers)
    for u in range(GY):
        s["st"][u] = shrunk[3 * u : 3 * (u + 1)]
    copies = []
    for d in range(1, GY):
        peer = gy_peer(d)
        copy = remote(s["st"].at[peer[1]], s["f2"].at[gy], s["bs"].at[d - 1], s["br"].at[d - 1], peer)
        copy.start()
        copies.append(copy)
    s["f2"][gy] = s["st"][gy]
    for copy in copies:
        copy.wait_recv()
    tiles = [s["f2"][:, a, 128 * c : 128 * (c + 1)] for a in range(3) for c in range(3)]
    tiles += [jnp.zeros((GY, 128), jnp.float32)] * 7
    return jnp.concatenate(swap_granules(tiles), axis=0), copies


def spread_core(basis, columns, out_ref, s):
    gx, gy, *_ = place()
    row, half = lax.div(gy, 2), lax.rem(gy, 2)
    core = dot(basis, columns)
    for u in range(GY):
        s["cs"][u] = core[3 * u : 3 * (u + 1)]

    def copy(d):
        u = lax.bitwise_xor(gy, d)
        return remote(s["cs"].at[u], s["ro"].at[gx, half], s["ks"].at[d], s["kr"].at[gx, half], (row, u))

    @pl.when(row != gx)
    def _():
        copy(0).start()

    @pl.when(row == gx)
    def _():
        s["ro"][gx, half] = s["cs"][gy]

    for d in range(1, GY):
        copy(d).start()

    def arrival(k, h):
        source = lax.rem(gx + k, GX)
        return remote(s["cs"].at[0], s["ro"].at[source, h], s["ks"].at[0], s["kr"].at[source, h], (source, 2 * gx + h))

    for h in range(2):
        @pl.when(2 * gx + h != gy)
        def _(h=h):
            arrival(0, h).wait_recv()
        for k in range(1, GX):
            arrival(k, h).wait_recv()
    for h in range(2):
        tiles = swap_granules([s["ro"][g, h] for g in range(GX)])
        for a in range(3):
            for c in range(3):
                out_ref[3 * h + a, :, 128 * c : 128 * (c + 1)] = tiles[3 * a + c]

    @pl.when(row != gx)
    def _():
        copy(0).wait_send()

    for d in range(1, GY):
        copy(d).wait_send()


def greet_senders():
    gx, gy, *_ = place()
    barrier = pltpu.get_barrier_semaphore()
    for h in range(2):
        @pl.when(2 * gx + h != gy)
        def _(h=h):
            pl.semaphore_signal(barrier, inc=1, device_id=(gx, 2 * gx + h), device_id_type=MESH)
        for k in range(1, GX):
            pl.semaphore_signal(barrier, inc=1, device_id=(lax.rem(gx + k, GX), 2 * gx + h), device_id_type=MESH)


def await_everyone(count):
    gx, gy, *_ = place()

    @pl.when(lax.div(gy, 2) == gx)
    def _():
        await_greetings(count + 31)

    @pl.when(lax.div(gy, 2) != gx)
    def _():
        await_greetings(count + 32)


def whole_kernel(x_ref, start_one_ref, start_two_ref, one_ref, two_ref, core_ref, s):
    room = (s["g"], s["last"], s["inverse"])
    copies = gather_one(x_ref, s)
    flat = s["fib"][...].reshape(I1, COLS)
    gram_blocks(flat, s["one"]["gp"])
    all_reduce(s["one"]["gp"], s["one"]["total"], s["one"])
    refine_into(1.0 / (I2 * COLS), s["one"]["total"], start_one_ref, one_ref, *room)
    flat, more = gather_two(one_ref, flat, s)
    s["columns"][...] = flat
    gram_blocks(flat, s["two"]["gp"])
    all_reduce(s["two"]["gp"], s["two"]["total"], s["two"])
    refine_into(1.0 / (RANK * COLS), s["two"]["total"], start_two_ref, two_ref, *room)
    spread_core(two_ref[...], s["columns"][...], core_ref, s)
    for copy in copies + more:
        copy.wait_send()


WHOLE = dict(
    one=REDUCE, two=REDUCE,
    x=pltpu.VMEM((32, 16, COLS), jnp.float32), xc=DMA,
    xs=pltpu.VMEM((GX, 32, COLS), jnp.float32), fib=pltpu.VMEM((GX, 32, COLS), jnp.float32),
    st=pltpu.VMEM((GY, 3, COLS), jnp.float32), f2=pltpu.VMEM((GY, 3, COLS), jnp.float32),
    columns=pltpu.VMEM((I2, 128), jnp.float32),
    cs=pltpu.VMEM((GY, 3, 128), jnp.float32), ro=pltpu.VMEM((GX, 2, 3, 128), jnp.float32),
    g=pltpu.VMEM((I1, I1), jnp.float32), last=pltpu.VMEM((RANK, I1), jnp.float32),
    inverse=pltpu.VMEM((RANK, 128), jnp.float32),
    ks=DMA((32,)), kr=DMA((GX, 2)),
    bs=DMA((31,)), br=DMA((31,)), **{"as": DMA((2, 15)), "ar": DMA((2, 15))},
)

VMEM = pl.BlockSpec(memory_space=pltpu.VMEM)
ANY = pl.BlockSpec(memory_space=pltpu.HBM)


def exchange(kernel, name, ident, ins, outs, scratch):
    def body(*refs):
        count = len(refs) - 1
        kernel(*refs[:count], refs[count])

    def call(*args):
        single = len(outs) == 1
        shapes = [jax.ShapeDtypeStruct(o, jnp.float32) for o in outs]
        return pl.pallas_call(
            body,
            out_shape=shapes[0] if single else shapes,
            in_specs=ins,
            out_specs=VMEM if single else [VMEM] * len(outs),
            scratch_shapes=[scratch],
            compiler_params=pltpu.CompilerParams(
                collective_id=ident, has_side_effects=True, vmem_limit_bytes=32 * 1024 * 1024
            ),
            name=name,
        )(*args)

    return call


def dot(a, b, dims=((1,), (0,))):
    return lax.dot_general(a, b, (dims, ((), ())), precision=precise, preferred_element_type=jnp.float32)


def inverse_factor(c, beside=()):
    lane = lax.broadcasted_iota(jnp.int32, (8, 128), 1)
    row = lax.broadcasted_iota(jnp.int32, (8, 128), 0)
    tiles = [c[8 * i : 8 * (i + 1)] for i in range(RANK // 8)]
    result = []

    def spread_lane(tile, n):
        return jnp.broadcast_to(tile[:, n : n + 1], (8, 128))

    def spread_row(tile, n):
        return jnp.broadcast_to(tile[n : n + 1, :], (8, 128))

    last = RANK // 8 - 1
    own = [spread_lane(tiles[0], t) for t in range(8)]
    for k in range(RANK // 8):
        lo = 8 * k
        near = min(k + 2, last)
        inside = (lane >= lo) & (lane < lo + 8)
        y = [[spread_lane(tiles[i], lo + t) for t in range(8)] for i in range(k + 1, near + 1)]
        if k < last:
            coming = [spread_lane(tiles[k + 1], lo + 8 + t) for t in range(8)]
        d = [[spread_row(own[t], s) for t in range(s + 1)] for s in range(8)]
        unit = jnp.where(inside, jnp.where(lane - lo == row, 1.0, 0.0), tiles[k])
        p = [spread_row(unit, s) for s in range(8)]
        if k in (2, 6) and beside:
            beside[(2, 6).index(k)]()
        rd = [None] * 8
        m = [[None] * 8 for _ in range(8)]
        for t in range(8):
            rd[t] = 1.0 / d[t][t]
            for s in range(t + 1, 8):
                m[s][t] = d[s][t] * rd[t]
                for u in range(t + 1, s + 1):
                    d[s][u] = d[s][u] - m[s][t] * d[u][t]
                p[s] = p[s] - m[s][t] * p[t]
                for col in y:
                    col[s] = col[s] - m[s][t] * col[t]
        rows = p[0] * lax.rsqrt(d[0][0])
        for s in range(1, 8):
            rows = jnp.where(row == s, p[s] * lax.rsqrt(d[s][s]), rows)
        result.append(jnp.where(lane < lo + 8, rows, 0.0))
        if k == last:
            break
        scaled = [[col[t] * rd[t] for t in range(8)] for col in y]
        own = list(coming)
        for u in range(8):
            for t in range(8):
                own[u] = own[u] - scaled[0][t] * spread_row(y[0][t], u)
        if near < last:
            q = [p[t] * rd[t] for t in range(8)]
            for s in range(7, 0, -1):
                for t in range(s):
                    q[t] = q[t] - m[s][t] * q[s]
            picked = q[0]
            for t in range(1, 8):
                picked = jnp.where(row == t, q[t], picked)
            spread = [picked] if k == 0 else [jnp.zeros((lo, 128), jnp.float32), picked]
            spread = jnp.concatenate(spread + [jnp.zeros((120 - lo, 128), jnp.float32)], axis=0)
            change = dot(jnp.concatenate(tiles[near + 1 :], axis=0), spread)
        for i in range(k + 1, last + 1):
            new = jnp.where(inside, 0.0, tiles[i])
            if i <= near:
                for t in range(8):
                    new = new - scaled[i - k - 1][t] * p[t]
            else:
                at = 8 * (i - near - 1)
                new = new - change[at : at + 8]
            tiles[i] = new
    return jnp.concatenate(result, axis=0)


def refine_into(scale, blocks_ref, start_ref, out_ref, g_ref, last_ref, inverse_ref):
    for n, (p, q) in enumerate(BLOCKS):
        block = blocks_ref[128 * n : 128 * (n + 1)] * scale
        g_ref[128 * p : 128 * (p + 1), 128 * q : 128 * (q + 1)] = block
        if p != q:
            g_ref[128 * q : 128 * (q + 1), 128 * p : 128 * (p + 1)] = block.T
    pad = jnp.zeros((128 - RANK, 512), jnp.float32)

    def factor(images, beside=()):
        full = jnp.concatenate([images, pad], axis=0)
        return inverse_factor(dot(images, full, ((1,), (1,))), beside)

    def sweep(_, images):
        ahead = []

        def column(n):
            return lambda: ahead.append(dot(images, g_ref[:, 256 * n : 256 * (n + 1)]))

        inverse = factor(images, [column(n) for n in range(2)])
        last_ref[...] = images
        inverse_ref[...] = inverse
        return dot(inverse, jnp.concatenate([jnp.concatenate(ahead, axis=1), pad], axis=0))

    lax.fori_loop(0, ITERS, sweep, dot(start_ref[...], g_ref[...]))
    out_ref[...] = dot(inverse_ref[...], jnp.concatenate([last_ref[...], pad], axis=0))


def body(snapshot, start_one, start_two):
    start_two = start_two.reshape(GY, 16, RANK).transpose(2, 1, 0).reshape(RANK, I2)
    shapes = [(RANK, I1), (RANK, I2), (6, 3, COLS)]
    basis_one, basis_two, core_tensor = exchange(whole_kernel, "whole", 0, [ANY, VMEM, VMEM], shapes, WHOLE)(
        snapshot, start_one.T, start_two
    )
    basis_two = basis_two.reshape(RANK, 16, GY).transpose(2, 1, 0).reshape(I2, RANK)
    return (basis_one.T, basis_two, core_tensor)


def solution(mesh):
    in_specs = (P("gx", "gy", None), P(), P())
    out_specs = (P(), P(), P("gx", "gy", None))
    return jax.shard_map(body, mesh=mesh, in_specs=in_specs, out_specs=out_specs, check_vma=False)
```
